32 devices in a mesh: dp: 4 (over y, x), ctx: 8 (over z, core).
Axes of the slice: x: 2, y: 2, z: 4, core: 2. Of those that a mesh axis runs over, the one named last changes fastest.
Arguments:
- queries: bfloat16 [4, 1024, 1280], P('dp', 'ctx'), may hold values from -16 to 16
- keys: bfloat16 [4, 1024, 1280], P('dp', 'ctx'), may hold values from -16 to 16
- values: bfloat16 [4, 1024, 1280], P('dp', 'ctx'), may hold values from -6 to 6
- seg_lengths: int32 [4, 8], P('dp'), may hold values from 1 to 768, 1024 in all within a row
- out_grad: bfloat16 [4, 1024, 2560], P('dp', 'ctx'), may hold values from -6 to 6
- w_out: bfloat16 [1280, 2560], P('dp'), may hold values from -0.15625 to 0.15625
Outputs:
- attended: bfloat16 [4, 1024, 2560], P('dp', 'ctx')
- query_grad: bfloat16 [4, 1024, 1280], P('dp', 'ctx')
- key_grad: bfloat16 [4, 1024, 1280], P('dp', 'ctx')
- value_grad: bfloat16 [4, 1024, 1280], P('dp', 'ctx')
- w_out_grad: float32 [1280, 2560], P('dp')
The draws below stay inside these ranges and needn't reach their ends.
Inputs may be any that keep to these rules, and one draw needn't show every extreme that they name: `seg_lengths`: each record's lengths sum to 1024; the longest of each record is exactly 768.
All inputs are finite; a program needn't handle non-finite values.
Results may differ from the reference program's by a relative error of at most 0.027.
Values may be sent and summed in bfloat16 or wider, within the bound.
A program may use at most 192 MiB of HBM per device.

```python
import math
import jax
import jax.numpy as jnp
import numpy as np
from jax import lax

D = 2560
HEADS = 10
HD = 128
NSEG = 8
INNER = 1280
SEQ = 1024
SEG_MOST = 768
BATCH = 4


def base_rows(key, spread_low, spread_high, factor):
    row_scale = jnp.exp(jax.random.uniform(jax.random.fold_in(key, 31), (BATCH, SEQ, HEADS, 1), minval=math.log(spread_low), maxval=math.log(spread_high)))
    entries = jnp.clip(jax.random.normal(jax.random.fold_in(key, 32), (BATCH, SEQ, HEADS, HD)), -4.0, 4.0)
    return factor * row_scale * entries


def draw_queries(key, part):
    base = base_rows(jax.random.fold_in(key, 41), 0.5, 2.0, 0.8)
    result = base
    return result.reshape(BATCH, SEQ, HEADS * HD).astype(jnp.bfloat16)


def draw_keys(key, part):
    base = base_rows(jax.random.fold_in(key, 42), 0.3, 3.0, 1.0)
    result = base
    return result.reshape(BATCH, SEQ, HEADS * HD).astype(jnp.bfloat16)


def steps_of(key, shape, split, least, largest):
    level = 1.0
    for dim, parts in split:
        draws = jax.random.uniform(jax.random.fold_in(jax.random.fold_in(key, 6), dim), (parts,), jnp.float32, least / len(split), largest / len(split))
        level = level * jnp.repeat(jnp.exp(draws), shape[dim] // parts).reshape((-1,) + (1,) * (len(shape) - 1 - dim))
    return level


def length_profile(number_of, total, bound, lean):
    weights = [(1 << 20) // math.isqrt(grade ** lean) + 1 for grade in range(2, number_of + 1)]
    surplus, holding = total - bound - (number_of - 1), [1] * (number_of - 1)
    while surplus > 0:
        movable = [i for i in range(number_of - 1) if holding[i] < bound]
        whole, budget = sum([weights[i] for i in movable]), surplus
        for i in movable:
            more = min(bound - holding[i], max(1, budget * weights[i] // whole), surplus)
            holding[i] = holding[i] + more
            surplus = surplus - more
    return np.array([bound] + holding)


def uneven(rng, count, total, limit, lean):
    if count == 2:
        one = jax.random.randint(rng, (), max(1, total - limit), min(limit, total - 1) + 1)
        return jnp.stack([one, total - one])
    tallies = jnp.asarray(length_profile(count, total, limit, lean), jnp.int32)
    pairs = (count - 1) // 2
    giver, sink = tallies[1:1 + 2 * pairs:2], tallies[2:2 + 2 * pairs:2]
    slack = jnp.minimum(giver - 1, limit - sink)
    shifted = jax.random.randint(jax.random.fold_in(rng, 1), (pairs,), 0, 1 << 20) % (slack + 1)
    tallies = tallies.at[1:1 + 2 * pairs:2].set(giver - shifted).at[2:2 + 2 * pairs:2].set(sink + shifted)
    return tallies[jax.random.permutation(jax.random.fold_in(rng, 2), count)]


def normal_values(rng, extent, scale, reach, shards=(), kind=jnp.bfloat16):
    array = jax.random.normal(rng, extent, jnp.float32) * scale
    if len(shards) > 0:
        array = steps_of(rng, extent, shards, -0.22, 0.18) * array
    return jnp.clip(array, min=-reach, max=reach).astype(kind)


def setup_inputs(seed: int = 0) -> dict:
    key_list = jax.random.split(jax.random.key(seed), 7)
    return {
        "queries": draw_queries(jax.random.fold_in(key_list[6], 71), 0),
        "keys": draw_keys(jax.random.fold_in(key_list[6], 71), 0),
        "values": normal_values(key_list[2], (BATCH, SEQ, INNER), 1.0, 6.0, ((0, 4), (1, 8))),
        "seg_lengths": jax.vmap(lambda own: uneven(own, NSEG, SEQ, SEG_MOST, 2))(jax.random.split(key_list[3], BATCH)).reshape((BATCH, NSEG)).astype(jnp.int32),
        "out_grad": normal_values(key_list[4], (BATCH, SEQ, D), 1.0, 6.0, ((0, 4), (1, 8))),
        "w_out": normal_values(key_list[5], (INNER, D), INNER ** -0.5, 0.15625, ((0, 4),)),
    }


MASKED_SCORE = -1e+30

def segment_ids(length_row):
    segment_ends = jnp.cumsum(length_row).astype(jnp.int32)
    positions = jnp.arange(SEQ, dtype=jnp.int32)
    return lax.optimization_barrier(jnp.sum((segment_ends[None, :] <= positions[:, None]).astype(jnp.int32), axis=1))

def one_head(operands):
    query_head, key_head, value_head, grad_head, segments = operands
    score_scale = 1.0 / math.sqrt(HD)
    block_rows = min(SEQ, 512)
    block_count = SEQ // block_rows

    def block_scores(first_row):
        query_block = lax.dynamic_slice_in_dim(query_head, first_row, block_rows, 0)
        scores = jnp.dot(query_block, key_head.T, preferred_element_type=jnp.float32) * score_scale
        query_segments = lax.dynamic_slice_in_dim(segments, first_row, block_rows, 0)
        return (scores, query_segments[:, None] == segments[None, :])

    def forward(block_index):
        first_row = block_index * block_rows
        scores, same_segment = block_scores(first_row)
        row_max = lax.optimization_barrier(jnp.max(jnp.where(same_segment, scores, MASKED_SCORE), axis=1))
        row_sum = lax.optimization_barrier(jnp.sum(jnp.where(same_segment, jnp.exp(scores - row_max[:, None]), 0.0), axis=1))
        log_norm = row_max + jnp.log(row_sum)
        probs = jnp.where(same_segment, jnp.exp(scores - log_norm[:, None]), 0.0)
        attention = jnp.dot(probs.astype(jnp.bfloat16), value_head, preferred_element_type=jnp.float32)
        return (attention.astype(jnp.bfloat16), log_norm)
    attention, log_norm = lax.map(forward, jnp.arange(block_count, dtype=jnp.int32))
    attention = attention.reshape(SEQ, HD)
    log_norm = log_norm.reshape(SEQ)
    grad_dot = lax.optimization_barrier(jnp.sum(grad_head.astype(jnp.float32) * attention.astype(jnp.float32), axis=1))

    def backward(carried, block_index):
        key_sum, value_sum = carried
        first_row = block_index * block_rows
        scores, same_segment = block_scores(first_row)
        query_block = lax.dynamic_slice_in_dim(query_head, first_row, block_rows, 0)
        grad_block = lax.dynamic_slice_in_dim(grad_head, first_row, block_rows, 0)
        norm_block = lax.dynamic_slice_in_dim(log_norm, first_row, block_rows, 0)
        dot_block = lax.dynamic_slice_in_dim(grad_dot, first_row, block_rows, 0)
        probs = jnp.where(same_segment, jnp.exp(scores - norm_block[:, None]), 0.0)
        probs_b = probs.astype(jnp.bfloat16)
        dprob = jnp.dot(grad_block, value_head.T, preferred_element_type=jnp.float32)
        dscore_b = (probs * (dprob - dot_block[:, None])).astype(jnp.bfloat16)
        query_part = jnp.dot(dscore_b, key_head, preferred_element_type=jnp.float32) * score_scale
        key_sum = key_sum + jnp.dot(dscore_b.T, query_block, preferred_element_type=jnp.float32)
        value_sum = value_sum + jnp.dot(probs_b.T, grad_block, preferred_element_type=jnp.float32)
        return ((key_sum, value_sum), query_part.astype(jnp.bfloat16))
    zeros = jnp.zeros((SEQ, HD), jnp.float32)
    (key_sum, value_sum), query_part = lax.scan(backward, (zeros, zeros), jnp.arange(block_count, dtype=jnp.int32))
    key_part = (key_sum * score_scale).astype(jnp.bfloat16)
    return (attention, query_part.reshape(SEQ, HD), key_part, value_sum.astype(jnp.bfloat16))

def split_heads(matrix):
    return matrix.reshape(BATCH, SEQ, HEADS, HD).transpose(0, 2, 1, 3).reshape(BATCH * HEADS, SEQ, HD)

def merge_heads(matrix):
    return matrix.reshape(BATCH, HEADS, SEQ, HD).transpose(0, 2, 1, 3).reshape(BATCH, SEQ, INNER)

def reference(queries, keys, values, seg_lengths, out_grad, w_out):
    flat_grad = out_grad.reshape(BATCH * SEQ, D)
    attn_grad = jnp.dot(flat_grad, w_out.T, preferred_element_type=jnp.float32).astype(jnp.bfloat16)
    attn_grad = attn_grad.reshape(BATCH, SEQ, INNER)
    segments = jax.vmap(segment_ids)(seg_lengths)
    segments = jnp.repeat(segments, HEADS, axis=0)
    operands = (split_heads(queries), split_heads(keys), split_heads(values), split_heads(attn_grad), segments)
    attention, query_part, key_part, value_part = lax.map(one_head, operands)
    attention = merge_heads(attention)
    flat_attention = attention.reshape(BATCH * SEQ, INNER)
    attended = jnp.dot(flat_attention, w_out, preferred_element_type=jnp.float32).astype(jnp.bfloat16)
    w_out_grad = jnp.dot(flat_attention.T, flat_grad, preferred_element_type=jnp.float32)
    return (attended.reshape(BATCH, SEQ, D), merge_heads(query_part), merge_heads(key_part), merge_heads(value_part), w_out_grad)
```

```python
import functools
import math

import jax
import jax.numpy as jnp
from jax import lax
from jax.experimental import pallas as pl
from jax.experimental.pallas import tpu as pltpu
from jax.sharding import PartitionSpec as P

HEADS = 10
HD = 128
MASKED_SCORE = -1e30
MESH = pl.DeviceIdType.MESH
BF16 = jnp.bfloat16
F32 = jnp.float32
VMEM_BYTES = 56 * 1024 * 1024


def owner_of(head, n):
    slot, place = divmod(head, n)
    if slot and 2 * place + 2 < n:
        place = 2 * place + 2
    return place, slot


def head_in_slot(me, slot, n):
    if slot == 0:
        return me, me < HEADS
    head, valid = 0, False
    for h in range(slot * n, min(HEADS, (slot + 1) * n)):
        place = owner_of(h, n)[0]
        head = jnp.where(me == place, h, head)
        valid = jnp.logical_or(valid, me == place)
    return head, valid


def dot_nt(a, b):
    return lax.dot_general(a, b, (((1,), (1,)), ((), ())), preferred_element_type=F32)


def dot_tn(a, b):
    return lax.dot_general(a, b, (((0,), (0,)), ((), ())), preferred_element_type=F32)


def dot_nn(a, b):
    return jnp.dot(a, b, preferred_element_type=F32)


def remote(src, dst, send, recv, dp, ctx):
    return pltpu.make_async_remote_copy(
        src_ref=src, dst_ref=dst, send_sem=send, recv_sem=recv, device_id=(dp, ctx), device_id_type=MESH
    )


def greet(n, ndp):
    me, dp = lax.axis_index("ctx"), lax.axis_index("dp")
    barrier = pltpu.get_barrier_semaphore()
    for down in range(ndp):
        for step in range(n):
            if down or step:
                pl.semaphore_signal(
                    barrier, inc=1, device_id=(lax.rem(dp + down, ndp), lax.rem(me + step, n)), device_id_type=MESH
                )
    pl.semaphore_wait(barrier, n * ndp - 1)


def whole_kernel(
    n, ndp, parts, block, span,
    seg_ref, q_ref, k_ref, v_ref, og_ref, w_ref,
    attended_ref, qg_ref, kg_ref, vg_ref, wg_ref,
    heads_ref, result_ref, probs_ref, dscore_ref, turned, query_mask, key_mask,
    w_pad, og_all, att_all, att_t, grad_ref, psend_buf, precv_buf, pown,
    xsend_buf, xrecv_buf, own_sum, chain_buf, outer_buf, middle_buf,
    send_sem, recv_sem, osend, orecv, gsend, grecv, asend, arecv, hsend, hrecv,
    psend, precv, xsend, xrecv, csend, crecv, mrecv, bsend, brecv, fsend, frecv,
):
    me, dp = lax.axis_index("ctx"), lax.axis_index("dp")
    core = lax.rem(me, 2)
    chip = me // 2
    chips = n // 2
    sibling = me + 1 - 2 * core
    slots, _, seq, _ = heads_ref.shape
    rows = q_ref.shape[0]
    width = og_ref.shape[1]
    wrows = w_ref.shape[0]
    half = wrows // 2
    wide = width // parts
    scale = 1.0 / math.sqrt(HD)
    my_rows = pl.ds(pl.multiple_of(me * rows, rows), rows)
    first = dp * wrows // HD
    lead = dp * wrows - first * HD
    greet(n, ndp)

    def record_rows(record):
        return pl.ds(pl.multiple_of(record * rows, rows), rows)

    def head_columns(head):
        if isinstance(head, int):
            return pl.ds(head * HD, HD)
        return pl.ds(pl.multiple_of(head * HD, HD), HD)

    def place_of(head):
        slot = head // n
        place = head - slot * n
        if slots > 1:
            moved = 2 * place + 2
            place = jnp.where(jnp.logical_and(slot > 0, moved < n), moved, place)
        return place, slot

    def low_source(head):
        return head * HD // wrows

    def high_source(head):
        return (head * HD + HD - 1) // wrows

    def send_head(tensor, source, head, start):
        place, slot = owner_of(head, n)
        columns = head_columns(head)
        copy = remote(
            source.at[:, columns], heads_ref.at[slot, tensor, my_rows],
            send_sem.at[tensor, head], recv_sem.at[slot, tensor], dp, place,
        )

        @pl.when(me != place)
        def _():
            if start:
                copy.start()
            else:
                copy.wait_send()

        if start:
            @pl.when(me == place)
            def _():
                heads_ref[slot, tensor, my_rows, :] = source[:, columns]

    def await_head(slot, tensor):
        waited = heads_ref.at[slot, tensor, pl.ds(0, rows * (n - 1))]
        pltpu.make_async_copy(waited, waited, recv_sem.at[slot, tensor]).wait()

    def og_copy(source, at, count, record, sem, slot, peer):
        landed = pl.ds(pl.multiple_of(record * rows + at, 16), count)
        return remote(source, og_all.at[landed], osend.at[sem], orecv.at[slot], peer, me)

    spread = []
    if ndp == 4:
        cut = rows // 2
        across = dp + 1 - 2 * lax.rem(dp, 2)
        along = lax.rem(dp + 2, 4)
        corner = 3 - dp
        peers = (across, along, corner)
        for order in range(2):
            for axis, peer in enumerate((across, along)):
                part = order if axis == 0 else 1 - order
                copy = og_copy(og_ref.at[pl.ds(part * cut, cut)], part * cut, cut, dp, 2 * axis + part, 2 * axis + part, peer)
                copy.start()
                spread.append(copy)
    else:
        peers = tuple(lax.rem(dp + ndp - step, ndp) for step in range(1, ndp))
        for step in range(1, ndp):
            copy = og_copy(og_ref, 0, rows, dp, step, step, lax.rem(dp + step, ndp))
            copy.start()
            spread.append(copy)

    for tensor, source in enumerate((q_ref, k_ref, v_ref)):
        for head in range(HEADS):
            send_head(tensor, source, head, True)

    w_pad[...] = jnp.zeros_like(w_pad)
    w_pad[pl.ds(pl.multiple_of(lead, 16), wrows), :] = w_ref[...]
    og_all[record_rows(dp), :] = og_ref[...]

    def grad_copy(step, record, spot):
        head = first + spot
        place, slot = place_of(head)
        which = dp - low_source(head)
        return remote(
            grad_ref.at[step, :, head_columns(spot)], heads_ref.at[slot, 3 + which, my_rows],
            gsend.at[step, spot], grecv.at[slot, which], record, place,
        )

    def make_grad(step, record):
        grad_ref[step] = dot_nt(og_all[record_rows(record), :], w_pad[...]).astype(BF16)
        for spot in range(span):
            if step:
                grad_copy(step, record, spot).start()
            else:
                place, slot = place_of(first + spot)

                @pl.when(place == me)
                def _():
                    heads_ref[slot, 3 + dp - low_source(first + spot), my_rows, :] = grad_ref[0, :, head_columns(spot)]

                @pl.when(place != me)
                def _():
                    grad_copy(0, record, spot).start()

    make_grad(0, dp)

    @pl.loop(0, seq // block)
    def _(index):
        at = pl.ds(pl.multiple_of(index * block, block), block)
        position = lax.broadcasted_iota(jnp.int32, (block, HD), 0) + index * block
        lane = lax.broadcasted_iota(jnp.int32, (block, HD), 1)
        count = seg_ref.shape[1]
        end = jnp.int32(0)
        segment = jnp.zeros((block, HD), jnp.int32)
        for i in range(count):
            end = end + seg_ref[0, i]
            segment = segment + jnp.where(position >= end, 1, 0)
        query_mask[at, :] = jnp.where(segment == lane, 1.0, 0.0).astype(BF16)
        key_mask[at, :] = jnp.where(jnp.logical_or(segment == lane, lane >= count), 0.0, MASKED_SCORE).astype(BF16)

    def await_og(slot, at, count, record):
        landed = og_all.at[pl.ds(pl.multiple_of(record * rows + at, 16), count)]
        remote(landed, landed, osend.at[0], orecv.at[slot], dp, me).wait_recv()
        return landed

    if ndp == 4:
        for axis, (peer, other) in enumerate(((across, along), (along, across))):
            landed = await_og(3 * axis, axis * cut, cut, peer)
            copy = og_copy(landed, axis * cut, cut, peer, 4 + axis, 4 + axis, other)
            copy.start()
            spread.append(copy)
        for axis, peer in enumerate((across, along)):
            await_og(axis + 1, (1 - axis) * cut, cut, peer)
            make_grad(axis + 1, peer)
        for axis in range(2):
            await_og(4 + axis, axis * cut, cut, corner)
        make_grad(3, corner)
    else:
        for step, peer in enumerate(peers, 1):
            await_og(step, 0, rows, peer)
            make_grad(step, peer)

    def attention_copy(slot, step, which):
        head, _ = head_in_slot(me, slot, n)
        other = lax.rem(me + step, n)
        target = low_source(head) + which
        spot = head - target * wrows // HD
        source = result_ref.at[slot, 0, pl.ds(pl.multiple_of(other * rows, rows), rows)]
        return target, spot, remote(
            source, att_all.at[record_rows(dp), head_columns(spot)],
            asend.at[slot, step, which], arecv.at[dp, spot], target, other,
        )

    def attention_copies(slot, start):
        head, _ = head_in_slot(me, slot, n)
        for which in range(2):
            @pl.when(low_source(head) + which <= high_source(head))
            def _():
                for step in range(n):
                    target, spot, copy = attention_copy(slot, step, which)

                    def act():
                        if start:
                            copy.start()
                        else:
                            copy.wait_send()

                    if step:
                        act()
                    else:
                        pl.when(target != dp)(act)
                        if start:
                            @pl.when(target == dp)
                            def _():
                                att_all[record_rows(dp), head_columns(spot)] = result_ref[slot, 0, my_rows, :]

    log2e = math.log2(math.e)
    for slot in range(slots):
        @pl.when(head_in_slot(me, slot, n)[1])
        def _():
            for tensor in range(3):
                await_head(slot, tensor)
            turned[...] = heads_ref[slot, 2].T

            @pl.loop(0, seq // block)
            def _(index):
                at = pl.ds(pl.multiple_of(index * block, block), block)
                left = jnp.concatenate([heads_ref[slot, 1], key_mask[...]], axis=1)
                right = jnp.concatenate([heads_ref[slot, 0, at, :], query_mask[at, :]], axis=1)
                scores = dot_nt(left, right)
                top = jnp.max(scores, axis=0, keepdims=True)
                shifted = jnp.exp2((scores - top) * (scale * log2e))
                total = jnp.sum(shifted, axis=0, keepdims=True)
                probs_b = (shifted * (1.0 / total)).astype(BF16)
                probs_ref[slot, :, at] = probs_b
                result_ref[slot, 0, at, :] = dot_nn(turned[...], probs_b).astype(BF16).T

            attention_copies(slot, True)

    targets = (None, qg_ref, kg_ref, vg_ref)

    def home_copy(slot, tensor, step):
        head, _ = head_in_slot(me, slot, n)
        other = lax.rem(me + step, n)
        source = result_ref.at[slot, tensor, pl.ds(pl.multiple_of(other * rows, rows), rows)]
        return remote(
            source, targets[tensor].at[:, head_columns(head)],
            hsend.at[tensor, slot, step], hrecv.at[tensor, head], dp, other,
        )

    def send_home(slot, tensor):
        head, _ = head_in_slot(me, slot, n)
        for step in range(1, n):
            home_copy(slot, tensor, step).start()
        targets[tensor][:, head_columns(head)] = result_ref[slot, tensor, my_rows, :]

    def receive_home(tensor):
        for head in range(HEADS):
            place, _ = owner_of(head, n)

            @pl.when(me != place)
            def _():
                landed = targets[tensor].at[:, head_columns(head)]
                remote(landed, landed, hsend.at[tensor, 0, 0], hrecv.at[tensor, head], dp, place).wait_recv()

    for slot in range(slots):
        @pl.when(head_in_slot(me, slot, n)[1])
        def _():
            head, _ = head_in_slot(me, slot, n)
            turned[...] = heads_ref[slot, 1].T
            for which in range(2):
                source = low_source(head) + which

                def await_grad(count):
                    waited = heads_ref.at[slot, 3 + which, pl.ds(0, rows * count)]
                    pltpu.make_async_copy(waited, waited, grecv.at[slot, which]).wait()

                @pl.when(source <= high_source(head))
                def _():
                    pl.when(source == dp)(lambda: await_grad(n - 1))
                    pl.when(source != dp)(lambda: await_grad(n))
                    if which:
                        heads_ref[slot, 3] = heads_ref[slot, 3] + heads_ref[slot, 4]

            @pl.loop(0, seq // block)
            def _(index):
                at = pl.ds(pl.multiple_of(index * block, block), block)
                result_ref[slot, 3, at, :] = dot_nn(probs_ref[slot, at, :], heads_ref[slot, 3]).astype(BF16)

            send_home(slot, 3)

            @pl.loop(0, seq // block)
            def _(index):
                at = pl.ds(pl.multiple_of(index * block, block), block)
                grad = heads_ref[slot, 3, at, :]
                product = grad.astype(F32) * result_ref[slot, 0, at, :].astype(F32)
                grad_dot = jnp.sum(product.T, axis=0, keepdims=True)
                dprob = dot_nt(heads_ref[slot, 2], grad)
                dscore = (probs_ref[slot, :, at].astype(F32) * (dprob - grad_dot)).astype(BF16)
                dscore_ref[:, at] = dscore
                result_ref[slot, 1, at, :] = (dot_nn(turned[...], dscore) * scale).astype(BF16).T

            send_home(slot, 1)

            @pl.loop(0, seq // block)
            def _(index):
                at = pl.ds(pl.multiple_of(index * block, block), block)
                result_ref[slot, 2, at, :] = (dot_nn(dscore_ref[at, :], heads_ref[slot, 0]) * scale).astype(BF16)

            send_home(slot, 2)

    for record in range(ndp):
        for spot in range(span):
            landed = att_all.at[record_rows(record), head_columns(spot)]
            here = jnp.logical_and(record == dp, place_of(first + spot)[0] == me)

            @pl.when(jnp.logical_not(here))
            def _():
                remote(landed, landed, asend.at[0, 0, 0], arecv.at[record, spot], dp, sibling).wait_recv()

    def part_columns(part):
        return pl.ds(part * wide, wide)

    def share(which):
        return pl.ds(pl.multiple_of(lead + which * half, 16), half)

    def pair_copy(part):
        columns = part_columns(part)
        return remote(
            xsend_buf.at[:, columns], xrecv_buf.at[:, columns], xsend.at[part], xrecv.at[part], dp, sibling,
        )

    def partial_copy(part, step):
        columns = part_columns(part)
        other = lax.rem(dp + step, ndp)
        return remote(
            psend_buf.at[record_rows(other), columns], precv_buf.at[step, :, columns],
            psend.at[part, step], precv.at[part, step], other, me,
        )

    att_t[...] = att_all[...].T
    for part in range(parts):
        columns = part_columns(part)
        xsend_buf[:, columns] = dot_nn(att_t[share(1 - core), :], og_all[:, columns]).astype(BF16)
        pair_copy(part).start()
    for part in range(parts):
        columns = part_columns(part)
        psend_buf[:, columns] = dot_nn(att_all[...], w_pad[:, columns]).astype(BF16)
        for step in range(1, ndp):
            partial_copy(part, step).start()

    my_half = pl.ds(pl.multiple_of(core * half, 16), half)
    their_half = pl.ds(pl.multiple_of((1 - core) * half, 16), half)
    depth = jnp.where(chip < chips // 2, chip, chips - 1 - chip)
    toward = jnp.where(chip < chips // 2, 1, -1)
    innermost = depth == chips // 2 - 1
    inner = me + 2 * toward
    outer = me - 2 * toward

    def inward_copy(part):
        columns = part_columns(part)
        return remote(
            chain_buf.at[:, columns], outer_buf.at[:, columns], csend.at[part], crecv.at[part], dp, inner,
        )

    def middle_copy(part):
        columns = part_columns(part)
        return remote(
            chain_buf.at[:, columns], middle_buf.at[:, columns], csend.at[part], mrecv.at[part], dp, inner,
        )

    def outward_copy(part):
        landed = wg_ref.at[my_half, part_columns(part)]
        return remote(landed, landed, bsend.at[part], brecv.at[part], dp, outer)

    def pass_copy(part, held):
        landed = wg_ref.at[held, part_columns(part)]
        return remote(landed, landed, fsend.at[part], frecv.at[part], dp, sibling)

    def finish(part):
        columns = part_columns(part)

        @pl.when(innermost)
        def _():
            middle_copy(part).wait_recv()
            total = chain_buf[:, columns].astype(F32) + middle_buf[:, columns].astype(F32)
            wg_ref[my_half, columns] = total.astype(BF16)

        @pl.when(jnp.logical_not(innermost))
        def _():
            outward_copy(part).wait_recv()

        @pl.when(depth > 0)
        def _():
            outward_copy(part).start()

        pass_copy(part, my_half).start()

    for part in range(parts):
        columns = part_columns(part)
        own_sum[...] = dot_nn(att_t[share(core), :], og_all[:, columns])
        pair_copy(part).wait_recv()
        own_sum[...] += xrecv_buf[:, columns].astype(F32)

        @pl.when(depth > 0)
        def _():
            inward_copy(part).wait_recv()
            own_sum[...] += outer_buf[:, columns].astype(F32)

        chain_buf[:, columns] = own_sum[...].astype(BF16)

        @pl.when(innermost)
        def _():
            middle_copy(part).start()

        @pl.when(jnp.logical_not(innermost))
        def _():
            inward_copy(part).start()

        if part:
            finish(part - 1)
    finish(parts - 1)

    for part in range(parts):
        columns = part_columns(part)
        total = psend_buf[record_rows(dp), columns].astype(F32)
        for step in range(1, ndp):
            partial_copy(part, step).wait_recv()
            total = total + precv_buf[step, :, columns].astype(F32)
        attended_ref[:, columns] = total.astype(BF16)

    for part in range(parts):
        pass_copy(part, their_half).wait_recv()
    for tensor in range(1, 4):
        receive_home(tensor)

    for tensor, source in enumerate((q_ref, k_ref, v_ref)):
        for head in range(HEADS):
            send_head(tensor, source, head, False)
    for copy in spread:
        copy.wait_send()
    for step, record in enumerate((dp,) + peers):
        for spot in range(span):
            copy = grad_copy(step, record, spot)
            if step:
                copy.wait_send()
            else:
                pl.when(place_of(first + spot)[0] != me)(copy.wait_send)
    for slot in range(slots):
        @pl.when(head_in_slot(me, slot, n)[1])
        def _():
            attention_copies(slot, False)
            for tensor in range(1, 4):
                for step in range(1, n):
                    home_copy(slot, tensor, step).wait_send()
    for part in range(parts):
        pair_copy(part).wait_send()
        for step in range(1, ndp):
            partial_copy(part, step).wait_send()
        inward_copy(part).wait_send()
        pl.when(depth > 0)(outward_copy(part).wait_send)
        pass_copy(part, my_half).wait_send()


def copy_kernel(*refs):
    sources, targets, held = refs[:5], refs[5:10], refs[10:15]
    wide_held, in_sem, out_sem = refs[15:]
    loads = [pltpu.make_async_copy(sources[i], held[i], in_sem.at[i]) for i in range(5)]
    stores = [
        pltpu.make_async_copy(held[i] if i < 4 else wide_held, targets[i], out_sem.at[i]) for i in range(5)
    ]
    for i in (4, 0, 1, 2, 3):
        loads[i].start()
    loads[4].wait()
    wide_held[...] = held[4][...].astype(F32)
    stores[4].start()
    for i in range(4):
        loads[i].wait()
        stores[i].start()
    for store in stores:
        store.wait()


def vmem(count):
    return [pl.BlockSpec(memory_space=pltpu.VMEM)] * count


def local(queries, keys, values, seg_lengths, out_grad, w_out):
    n, ndp = lax.axis_size("ctx"), lax.axis_size("dp")
    rows, inner = queries.shape[1:]
    width = out_grad.shape[2]
    seq = rows * n
    wrows = w_out.shape[0]
    half = wrows // 2
    slots = -(-HEADS // n)
    parts = 4
    wide = width // parts
    span = max(-(-(k + 1) * wrows // HD) - k * wrows // HD for k in range(ndp))
    shape = jax.ShapeDtypeStruct
    dma = pltpu.SemaphoreType.DMA
    out_shape = (
        shape((rows, width), BF16), shape((rows, inner), BF16), shape((rows, inner), BF16),
        shape((rows, inner), BF16), shape((wrows, width), F32),
    )
    outputs = pl.pallas_call(
        functools.partial(whole_kernel, n, ndp, parts, 256, span),
        out_shape=out_shape[:4] + (shape((wrows, width), BF16),),
        in_specs=[pl.BlockSpec(memory_space=pltpu.SMEM)] + vmem(5),
        out_specs=tuple(vmem(5)),
        scratch_shapes=[
            pltpu.VMEM((slots, 5, seq, HD), BF16),
            pltpu.VMEM((slots, 4, seq, HD), BF16),
            pltpu.VMEM((slots, seq, seq), BF16),
            pltpu.VMEM((seq, seq), BF16),
            pltpu.VMEM((HD, seq), BF16),
            pltpu.VMEM((seq, HD), BF16),
            pltpu.VMEM((seq, HD), BF16),
            pltpu.VMEM((span * HD, width), BF16),
            pltpu.VMEM((ndp * rows, width), BF16),
            pltpu.VMEM((ndp * rows, span * HD), BF16),
            pltpu.VMEM((span * HD, ndp * rows), BF16),
            pltpu.VMEM((ndp, rows, span * HD), BF16),
            pltpu.VMEM((ndp * rows, width), BF16),
            pltpu.VMEM((ndp, rows, width), BF16),
            pltpu.VMEM((8, HD), F32),
            pltpu.VMEM((half, width), BF16),
            pltpu.VMEM((half, width), BF16),
            pltpu.VMEM((half, wide), F32),
            pltpu.VMEM((half, width), BF16),
            pltpu.VMEM((half, width), BF16),
            pltpu.VMEM((half, width), BF16),
            dma((3, HEADS)), dma((slots, 3)), dma((max(ndp, 6),)), dma((max(ndp, 6),)),
            dma((ndp, span)), dma((slots, 2)), dma((slots, n, 2)), dma((ndp, span)),
            dma((4, slots, n)), dma((4, HEADS)),
            dma((parts, ndp)), dma((parts, ndp)), dma((parts,)), dma((parts,)),
            dma((parts,)), dma((parts,)), dma((parts,)), dma((parts,)), dma((parts,)), dma((parts,)), dma((parts,)),
        ],
        compiler_params=pltpu.CompilerParams(
            collective_id=0, has_side_effects=True, vmem_limit_bytes=VMEM_BYTES
        ),
    )(seg_lengths, queries[0], keys[0], values[0], out_grad[0], w_out)
    anywhere = [pl.BlockSpec(memory_space=pl.ANY)] * 5
    attended, query_grad, key_grad, value_grad, weight_grad = pl.pallas_call(
        copy_kernel,
        out_shape=out_shape,
        in_specs=anywhere,
        out_specs=tuple(anywhere),
        scratch_shapes=[pltpu.VMEM(x.shape, BF16) for x in out_shape]
        + [pltpu.VMEM((wrows, width), F32), dma((5,)), dma((5,))],
        compiler_params=pltpu.CompilerParams(vmem_limit_bytes=VMEM_BYTES),
    )(*outputs)
    return (attended[None], query_grad[None], key_grad[None], value_grad[None], weight_grad)


def solution(mesh):
    in_specs = (
        P("dp", "ctx", None),
        P("dp", "ctx", None),
        P("dp", "ctx", None),
        P("dp", None),
        P("dp", "ctx", None),
        P("dp", None),
    )
    out_specs = (
        P("dp", "ctx", None),
        P("dp", "ctx", None),
        P("dp", "ctx", None),
        P("dp", "ctx", None),
        P("dp", None),
    )
    return jax.shard_map(local, mesh=mesh, in_specs=in_specs, out_specs=out_specs, check_vma=False)
```

```python
import functools
import math

import jax
import jax.numpy as jnp
from jax import lax
from jax.experimental import pallas as pl
from jax.experimental.pallas import tpu as pltpu
from jax.sharding import PartitionSpec as P

HEADS = 10
HD = 128
MASKED_SCORE = -1e30
MESH = pl.DeviceIdType.MESH
BF16 = jnp.bfloat16
F32 = jnp.float32
VMEM_BYTES = 56 * 1024 * 1024


def owner_of(head, n):
    slot, place = divmod(head, n)
    if slot and 2 * place + 2 < n:
        place = 2 * place + 2
    return place, slot


def head_in_slot(me, slot, n):
    if slot == 0:
        return me, me < HEADS
    head, valid = 0, False
    for h in range(slot * n, min(HEADS, (slot + 1) * n)):
        place = owner_of(h, n)[0]
        head = jnp.where(me == place, h, head)
        valid = jnp.logical_or(valid, me == place)
    return head, valid


def dot_nt(a, b):
    return lax.dot_general(a, b, (((1,), (1,)), ((), ())), preferred_element_type=F32)


def dot_tn(a, b):
    return lax.dot_general(a, b, (((0,), (0,)), ((), ())), preferred_element_type=F32)


def dot_nn(a, b):
    return jnp.dot(a, b, preferred_element_type=F32)


def remote(src, dst, send, recv, dp, ctx):
    return pltpu.make_async_remote_copy(
        src_ref=src, dst_ref=dst, send_sem=send, recv_sem=recv, device_id=(dp, ctx), device_id_type=MESH
    )


def greet(n, ndp):
    me, dp = lax.axis_index("ctx"), lax.axis_index("dp")
    barrier = pltpu.get_barrier_semaphore()
    for down in range(ndp):
        for step in range(n):
            if down or step:
                pl.semaphore_signal(
                    barrier, inc=1, device_id=(lax.rem(dp + down, ndp), lax.rem(me + step, n)), device_id_type=MESH
                )
    pl.semaphore_wait(barrier, n * ndp - 1)


def whole_kernel(
    n, ndp, parts, cuts, block, piece,
    seg_ref, q_ref, k_ref, v_ref, og_ref, w_hbm,
    attended_ref, qg_ref, kg_ref, vg_ref, wg_ref,
    heads_ref, grads_ref, attention_ref, result_ref, probs_ref, dscore_ref, turned, query_mask, key_mask,
    w_ref, og_all, att_t, att_all, grad_ref, psend_buf, precv_buf,
    xsend_buf, xrecv_buf, own_sum, chain_buf, outer_buf, middle_buf,
    load_sem, send_sem, recv_sem, osend, orecv, gsend, grecv, asend, arecv, hsend, hrecv,
    psend, precv, xsend, xrecv, csend, crecv, mrecv, bsend, brecv, fsend, frecv,
):
    me, dp = lax.axis_index("ctx"), lax.axis_index("dp")
    core = lax.rem(me, 2)
    chip = me // 2
    chips = n // 2
    sibling = me + 1 - 2 * core
    slots, _, seq, _ = heads_ref.shape
    rows = q_ref.shape[0]
    width = og_ref.shape[1]
    wrows = w_ref.shape[0]
    half = wrows // 2
    wide = width // parts
    broad = width // cuts
    pieces = wrows // piece
    scale = 1.0 / math.sqrt(HD)

    def record_rows(record):
        return pl.ds(pl.multiple_of(record * rows, rows), rows)

    my_rows = record_rows(me)
    loads = (
        pltpu.make_async_copy(w_hbm, w_ref, load_sem.at[0]),
        pltpu.make_async_copy(og_ref, og_all.at[record_rows(dp)], load_sem.at[1]),
    )
    for load in loads:
        load.start()
    greet(n, ndp)

    def head_columns(head):
        if isinstance(head, int):
            return pl.ds(head * HD, HD)
        return pl.ds(pl.multiple_of(head * HD, HD), HD)

    def place_of(head):
        slot = head // n
        place = head - slot * n
        if slots > 1:
            moved = 2 * place + 2
            place = jnp.where(jnp.logical_and(slot > 0, moved < n), moved, place)
        return place, slot

    def send_head(tensor, source, head, start):
        place, slot = owner_of(head, n)
        columns = head_columns(head)
        landing = heads_ref.at[slot, tensor, my_rows]
        copy = remote(
            source.at[:, columns], landing, send_sem.at[tensor, head], recv_sem.at[slot, tensor], dp, place,
        )

        @pl.when(me != place)
        def _():
            if start:
                copy.start()
            else:
                copy.wait_send()

        if start:
            @pl.when(me == place)
            def _():
                pltpu.make_async_copy(source.at[:, columns], landing, recv_sem.at[slot, tensor]).start()

    def await_head(slot, tensor):
        waited = heads_ref.at[slot, tensor]
        pltpu.make_async_copy(waited, waited, recv_sem.at[slot, tensor]).wait()

    def og_copy(source, at, count, record, slot, peer):
        landed = pl.ds(pl.multiple_of(record * rows + at, 16), count)
        return remote(source, og_all.at[landed], osend.at[slot], orecv.at[slot], peer, me)

    def send_slot(slot):
        for tensor, source in enumerate((q_ref, k_ref, v_ref)):
            for head in range(slot * n, min(HEADS, slot * n + n)):
                send_head(tensor, source, head, True)

    spread = []
    if ndp == 4:
        cut = rows // 2
        across = dp + 1 - 2 * lax.rem(dp, 2)
        along = lax.rem(dp + 2, 4)
        corner = 3 - dp
        peers = (across, along, corner)
        for order in range(2):
            for axis, peer in enumerate((across, along)):
                part = order if axis == 0 else 1 - order
                spread.append(
                    og_copy(og_ref.at[pl.ds(part * cut, cut)], part * cut, cut, dp, 2 * axis + part, peer)
                )
    else:
        peers = tuple(lax.rem(dp + ndp - step, ndp) for step in range(1, ndp))
        for step in range(1, ndp):
            spread.append(og_copy(og_ref, 0, rows, dp, step, lax.rem(dp + step, ndp)))
    for copy in spread:
        copy.start()
    send_slot(0)

    def piece_place(spot):
        feature = dp * wrows + spot * piece
        head = feature // HD
        place, slot = place_of(head)
        return place, slot, feature - head * HD

    def grad_copy(step, record, spot):
        place, slot, inside = piece_place(spot)
        return remote(
            grad_ref.at[step, pl.ds(spot * piece, piece)],
            grads_ref.at[slot, pl.ds(pl.multiple_of(inside, 16), piece), my_rows],
            gsend.at[step, spot], grecv.at[slot, inside // piece], record, place,
        )

    def make_grad(step, record):
        grad_ref[step] = dot_nt(w_ref[...], og_all[record_rows(record), :]).astype(BF16)
        for spot in range(pieces):
            if step:
                grad_copy(step, record, spot).start()
            else:
                place, slot, inside = piece_place(spot)

                @pl.when(place == me)
                def _():
                    held = pl.ds(pl.multiple_of(inside, 16), piece)
                    grads_ref[slot, held, my_rows] = grad_ref[0, pl.ds(spot * piece, piece), :]

                @pl.when(place != me)
                def _():
                    grad_copy(0, record, spot).start()

    for load in loads:
        load.wait()
    make_grad(0, dp)

    @pl.loop(0, seq // block)
    def _(index):
        at = pl.ds(pl.multiple_of(index * block, block), block)
        position = lax.broadcasted_iota(jnp.int32, (block, HD), 0) + index * block
        lane = lax.broadcasted_iota(jnp.int32, (block, HD), 1)
        count = seg_ref.shape[1]
        end = jnp.int32(0)
        segment = jnp.zeros((block, HD), jnp.int32)
        for i in range(count):
            end = end + seg_ref[0, i]
            segment = segment + jnp.where(position >= end, 1, 0)
        query_mask[at, :] = jnp.where(segment == lane, 1.0, 0.0).astype(BF16)
        key_mask[at, :] = jnp.where(jnp.logical_or(segment == lane, lane >= count), 0.0, MASKED_SCORE).astype(BF16)

    def await_og(slot, at, count, record):
        landed = og_all.at[pl.ds(pl.multiple_of(record * rows + at, 16), count)]
        remote(landed, landed, osend.at[0], orecv.at[slot], dp, me).wait_recv()
        return landed

    if ndp == 4:
        for axis, (peer, other) in enumerate(((across, along), (along, across))):
            landed = await_og(3 * axis, axis * cut, cut, peer)
            copy = og_copy(landed, axis * cut, cut, peer, 4 + axis, other)
            copy.start()
            spread.append(copy)
    for slot in range(1, slots):
        send_slot(slot)
    if ndp == 4:
        for axis, peer in enumerate((across, along)):
            await_og(axis + 1, (1 - axis) * cut, cut, peer)
            make_grad(axis + 1, peer)
    else:
        for step, peer in enumerate(peers, 1):
            await_og(step, 0, rows, peer)
            make_grad(step, peer)

    def attention_copy(slot, other, spot):
        head, _ = head_in_slot(me, slot, n)
        feature = head * HD + spot * piece
        target = feature // wrows
        row = feature - target * wrows
        landing = att_t.at[pl.ds(pl.multiple_of(row, 16), piece), record_rows(dp)]
        return target, landing, remote(
            attention_ref.at[slot, pl.ds(spot * piece, piece), record_rows(other)], landing,
            asend.at[slot, other, spot], arecv.at[dp, row // piece], target, other,
        )

    def attention_copies(slot, other, start):
        for spot in range(HD // piece):
            target, landing, copy = attention_copy(slot, other, spot)
            here = jnp.logical_and(target == dp, other == me)

            @pl.when(jnp.logical_not(here))
            def _():
                if start:
                    copy.start()
                else:
                    copy.wait_send()

            if start:
                @pl.when(here)
                def _():
                    landing[...] = attention_ref[slot, pl.ds(spot * piece, piece), my_rows]

    log2e = math.log2(math.e)

    def forward(slot):
        @pl.when(head_in_slot(me, slot, n)[1])
        def _():
            for tensor in range(3):
                await_head(slot, tensor)
            turned[...] = heads_ref[slot, 2].T

            @pl.loop(0, seq // block)
            def _(index):
                at = pl.ds(pl.multiple_of(index * block, block), block)
                left = jnp.concatenate([heads_ref[slot, 1], key_mask[...]], axis=1)
                right = jnp.concatenate([heads_ref[slot, 0, at, :], query_mask[at, :]], axis=1)
                scores = dot_nt(left, right)
                top = jnp.max(scores, axis=0, keepdims=True)
                shifted = jnp.exp2((scores - top) * (scale * log2e))
                total = jnp.sum(shifted, axis=0, keepdims=True)
                probs_b = (shifted * (1.0 / total)).astype(BF16)
                probs_ref[slot, :, at] = probs_b
                attention_ref[slot, :, at] = dot_nn(turned[...], probs_b).astype(BF16)
                for step in range(block // rows):
                    attention_copies(slot, index * (block // rows) + step, True)

    targets = (qg_ref, kg_ref, vg_ref)

    def home_copy(slot, tensor, other):
        head, _ = head_in_slot(me, slot, n)
        return remote(
            result_ref.at[slot, tensor, record_rows(other)], targets[tensor].at[:, head_columns(head)],
            hsend.at[tensor, slot, other], hrecv.at[tensor, head], dp, other,
        )

    def send_home(slot, tensor, other):
        @pl.when(other != me)
        def _():
            home_copy(slot, tensor, other).start()

        @pl.when(other == me)
        def _():
            head, _ = head_in_slot(me, slot, n)
            targets[tensor][:, head_columns(head)] = result_ref[slot, tensor, my_rows, :]

    def receive_home(tensor):
        for head in range(HEADS):
            place, _ = owner_of(head, n)

            @pl.when(me != place)
            def _():
                landed = targets[tensor].at[:, head_columns(head)]
                remote(landed, landed, hsend.at[tensor, 0, 0], hrecv.at[tensor, head], dp, place).wait_recv()

    def backward(slot):
        @pl.when(head_in_slot(me, slot, n)[1])
        def _():
            head, _ = head_in_slot(me, slot, n)
            turned[...] = heads_ref[slot, 1].T
            for spot in range(HD // piece):
                source = (head * HD + spot * piece) // wrows

                def await_grad(count):
                    waited = grads_ref.at[slot, pl.ds(spot * piece, piece), pl.ds(0, rows * count)]
                    pltpu.make_async_copy(waited, waited, grecv.at[slot, spot]).wait()

                pl.when(source == dp)(lambda: await_grad(n - 1))
                pl.when(source != dp)(lambda: await_grad(n))

            @pl.loop(0, seq // block)
            def _(index):
                at = pl.ds(pl.multiple_of(index * block, block), block)
                result_ref[slot, 2, at, :] = dot_nt(probs_ref[slot, at, :], grads_ref[slot]).astype(BF16)
                for step in range(block // rows):
                    send_home(slot, 2, index * (block // rows) + step)

            @pl.loop(0, seq // block)
            def _(index):
                at = pl.ds(pl.multiple_of(index * block, block), block)
                grad = grads_ref[slot, :, at]
                product = grad.astype(F32) * attention_ref[slot, :, at].astype(F32)
                grad_dot = jnp.sum(product, axis=0, keepdims=True)
                dprob = dot_nn(heads_ref[slot, 2], grad)
                dscore = (probs_ref[slot, :, at].astype(F32) * (dprob - grad_dot)).astype(BF16)
                dscore_ref[:, at] = dscore
                result_ref[slot, 0, at, :] = (dot_nn(turned[...], dscore) * scale).astype(BF16).T
                for step in range(block // rows):
                    send_home(slot, 0, index * (block // rows) + step)

            @pl.loop(0, seq // block)
            def _(index):
                at = pl.ds(pl.multiple_of(index * block, block), block)
                result_ref[slot, 1, at, :] = (dot_nn(dscore_ref[at, :], heads_ref[slot, 0]) * scale).astype(BF16)
                for step in range(block // rows):
                    send_home(slot, 1, index * (block // rows) + step)

    forward(0)
    if ndp == 4:
        for axis in range(2):
            await_og(4 + axis, axis * cut, cut, corner)
        make_grad(3, corner)
    for slot in range(1, slots):
        forward(slot)
    backward(0)

    for record in range(ndp):
        for spot in range(pieces):
            landed = att_t.at[pl.ds(spot * piece, piece), pl.ds(record * rows, rows)]
            here = jnp.logical_and(record == dp, piece_place(spot)[0] == me)

            @pl.when(jnp.logical_not(here))
            def _():
                remote(landed, landed, asend.at[0, 0, 0], arecv.at[record, spot], dp, sibling).wait_recv()

    def part_columns(part):
        return pl.ds(part * wide, wide)

    def cut_columns(part):
        return pl.ds(part * broad, broad)

    my_half = pl.ds(pl.multiple_of(core * half, 16), half)
    their_half = pl.ds(pl.multiple_of((1 - core) * half, 16), half)

    def pair_copy(part):
        columns = cut_columns(part)
        return remote(
            xsend_buf.at[:, columns], xrecv_buf.at[:, columns], xsend.at[part], xrecv.at[part], dp, sibling,
        )

    def partial_copy(part, step):
        columns = cut_columns(part)
        other = lax.rem(dp + step, ndp)
        return remote(
            psend_buf.at[record_rows(other), columns], precv_buf.at[step - 1, :, columns],
            psend.at[part, step], precv.at[part, step], other, me,
        )

    for part in range(cuts):
        columns = cut_columns(part)
        xsend_buf[:, columns] = dot_nn(att_t[their_half, :], og_all[:, columns]).astype(BF16)
        pair_copy(part).start()
    att_all[...] = att_t[...].T
    for part in range(cuts):
        columns = cut_columns(part)
        psend_buf[:, columns] = dot_nn(att_all[...], w_ref[:, columns]).astype(BF16)
        for step in range(1, ndp):
            partial_copy(part, step).start()
    for slot in range(1, slots):
        backward(slot)

    depth = jnp.where(chip < chips // 2, chip, chips - 1 - chip)
    toward = jnp.where(chip < chips // 2, 1, -1)
    innermost = depth == chips // 2 - 1
    inner = me + 2 * toward
    outer = me - 2 * toward

    def inward_copy(part):
        columns = part_columns(part)
        return remote(
            chain_buf.at[:, columns], outer_buf.at[:, columns], csend.at[part], crecv.at[part], dp, inner,
        )

    def middle_copy(part):
        columns = part_columns(part)
        return remote(
            chain_buf.at[:, columns], middle_buf.at[:, columns], csend.at[part], mrecv.at[part], dp, inner,
        )

    def outward_copy(part):
        landed = wg_ref.at[my_half, part_columns(part)]
        return remote(landed, landed, bsend.at[part], brecv.at[part], dp, outer)

    def pass_copy(part, held):
        landed = wg_ref.at[held, part_columns(part)]
        return remote(landed, landed, fsend.at[part], frecv.at[part], dp, sibling)

    def hand_on(part):
        @pl.when(depth > 0)
        def _():
            outward_copy(part).start()

        pass_copy(part, my_half).start()

    def finish_inner(part):
        @pl.when(innermost)
        def _():
            columns = part_columns(part)
            middle_copy(part).wait_recv()
            total = chain_buf[:, columns].astype(F32) + middle_buf[:, columns].astype(F32)
            wg_ref[my_half, columns] = total.astype(BF16)
            hand_on(part)

    lag = 2
    for part in range(parts):
        columns = part_columns(part)
        own_sum[...] = dot_nn(att_t[my_half, :], og_all[:, columns])
        if part * wide % broad == 0:
            pair_copy(part * wide // broad).wait_recv()
        own_sum[...] += xrecv_buf[:, columns].astype(F32)

        @pl.when(depth > 0)
        def _():
            inward_copy(part).wait_recv()
            own_sum[...] += outer_buf[:, columns].astype(F32)

        chain_buf[:, columns] = own_sum[...].astype(BF16)
        if part >= lag:
            inward_copy(part - lag).wait_send()

        @pl.when(innermost)
        def _():
            middle_copy(part).start()

        @pl.when(jnp.logical_not(innermost))
        def _():
            inward_copy(part).start()

        if part >= lag:
            finish_inner(part - lag)
    for part in range(parts - lag, parts):
        finish_inner(part)

    for part in range(cuts):
        columns = cut_columns(part)
        total = psend_buf[record_rows(dp), columns].astype(F32)
        for step in range(1, ndp):
            partial_copy(part, step).wait_recv()
            total = total + precv_buf[step - 1, :, columns].astype(F32)
        attended_ref[:, columns] = total.astype(BF16)

    for part in range(parts):
        @pl.when(jnp.logical_not(innermost))
        def _():
            outward_copy(part).wait_recv()
            hand_on(part)

    for tensor in range(3):
        receive_home(tensor)
    for part in range(parts):
        pass_copy(part, their_half).wait_recv()

    for tensor, source in enumerate((q_ref, k_ref, v_ref)):
        for head in range(HEADS):
            send_head(tensor, source, head, False)
    for copy in spread:
        copy.wait_send()
    for step, record in enumerate((dp,) + peers):
        for spot in range(pieces):
            copy = grad_copy(step, record, spot)
            if step:
                copy.wait_send()
            else:
                pl.when(piece_place(spot)[0] != me)(copy.wait_send)
    for slot in range(slots):
        @pl.when(head_in_slot(me, slot, n)[1])
        def _():
            for other in range(n):
                attention_copies(slot, other, False)
                for tensor in range(3):
                    pl.when(other != me)(home_copy(slot, tensor, other).wait_send)
    for part in range(cuts):
        pair_copy(part).wait_send()
        for step in range(1, ndp):
            partial_copy(part, step).wait_send()
    for part in range(parts):
        if part >= parts - lag:
            inward_copy(part).wait_send()
        pl.when(depth > 0)(outward_copy(part).wait_send)
        pass_copy(part, my_half).wait_send()


def copy_kernel(*refs):
    sources, targets, held = refs[:5], refs[5:10], refs[10:15]
    wide_held, in_sem, out_sem = refs[15:]
    loads = [pltpu.make_async_copy(sources[i], held[i], in_sem.at[i]) for i in range(5)]
    stores = [
        pltpu.make_async_copy(held[i] if i < 4 else wide_held, targets[i], out_sem.at[i]) for i in range(5)
    ]
    for i in (4, 0, 1, 2, 3):
        loads[i].start()
    loads[4].wait()
    wide_held[...] = held[4][...].astype(F32)
    stores[4].start()
    for i in range(4):
        loads[i].wait()
        stores[i].start()
    for store in stores:
        store.wait()


def vmem(count):
    return [pl.BlockSpec(memory_space=pltpu.VMEM)] * count


def local(queries, keys, values, seg_lengths, out_grad, w_out):
    n, ndp = lax.axis_size("ctx"), lax.axis_size("dp")
    rows, inner = queries.shape[1:]
    width = out_grad.shape[2]
    seq = rows * n
    wrows = w_out.shape[0]
    half = wrows // 2
    slots = -(-HEADS // n)
    parts, cuts = 10, 5
    wide = width // parts
    piece = math.gcd(HD, wrows)
    shape = jax.ShapeDtypeStruct
    dma = pltpu.SemaphoreType.DMA
    out_shape = (
        shape((rows, width), BF16), shape((rows, inner), BF16), shape((rows, inner), BF16),
        shape((rows, inner), BF16), shape((wrows, width), F32),
    )
    anywhere = [pl.BlockSpec(memory_space=pl.ANY)] * 5
    outputs = pl.pallas_call(
        functools.partial(whole_kernel, n, ndp, parts, cuts, 256, piece),
        out_shape=out_shape[:4] + (shape((wrows, width), BF16),),
        in_specs=[pl.BlockSpec(memory_space=pltpu.SMEM)] + anywhere,
        out_specs=tuple(vmem(5)),
        scratch_shapes=[
            pltpu.VMEM((slots, 3, seq, HD), BF16),
            pltpu.VMEM((slots, HD, seq), BF16),
            pltpu.VMEM((slots, HD, seq), BF16),
            pltpu.VMEM((slots, 3, seq, HD), BF16),
            pltpu.VMEM((slots, seq, seq), BF16),
            pltpu.VMEM((seq, seq), BF16),
            pltpu.VMEM((HD, seq), BF16),
            pltpu.VMEM((seq, HD), BF16),
            pltpu.VMEM((seq, HD), BF16),
            pltpu.VMEM((wrows, width), BF16),
            pltpu.VMEM((ndp * rows, width), BF16),
            pltpu.VMEM((wrows, ndp * rows), BF16),
            pltpu.VMEM((ndp * rows, wrows), BF16),
            pltpu.VMEM((ndp, wrows, rows), BF16),
            pltpu.VMEM((ndp * rows, width), BF16),
            pltpu.VMEM((ndp - 1, rows, width), BF16),
            pltpu.VMEM((half, width), BF16),
            pltpu.VMEM((half, width), BF16),
            pltpu.VMEM((half, wide), F32),
            pltpu.VMEM((half, width), BF16),
            pltpu.VMEM((half, width), BF16),
            pltpu.VMEM((half, width), BF16),
            dma((2,)), dma((3, HEADS)), dma((slots, 3)), dma((max(ndp, 6),)), dma((max(ndp, 6),)),
            dma((ndp, wrows // piece)), dma((slots, HD // piece)), dma((slots, n, HD // piece)), dma((ndp, wrows // piece)),
            dma((3, slots, n)), dma((3, HEADS)),
            dma((cuts, ndp)), dma((cuts, ndp)), dma((cuts,)), dma((cuts,)),
            dma((parts,)), dma((parts,)), dma((parts,)), dma((parts,)), dma((parts,)), dma((parts,)), dma((parts,)),
        ],
        compiler_params=pltpu.CompilerParams(
            collective_id=0, has_side_effects=True, vmem_limit_bytes=VMEM_BYTES
        ),
    )(seg_lengths, queries[0], keys[0], values[0], out_grad[0], w_out)
    attended, query_grad, key_grad, value_grad, weight_grad = pl.pallas_call(
        copy_kernel,
        out_shape=out_shape,
        in_specs=anywhere,
        out_specs=tuple(anywhere),
        scratch_shapes=[pltpu.VMEM(x.shape, BF16) for x in out_shape]
        + [pltpu.VMEM((wrows, width), F32), dma((5,)), dma((5,))],
        compiler_params=pltpu.CompilerParams(vmem_limit_bytes=VMEM_BYTES),
    )(*outputs)
    return (attended[None], query_grad[None], key_grad[None], value_grad[None], weight_grad)


def solution(mesh):
    in_specs = (
        P("dp", "ctx", None),
        P("dp", "ctx", None),
        P("dp", "ctx", None),
        P("dp", None),
        P("dp", "ctx", None),
        P("dp", None),
    )
    out_specs = (
        P("dp", "ctx", None),
        P("dp", "ctx", None),
        P("dp", "ctx", None),
        P("dp", "ctx", None),
        P("dp", None),
    )
    return jax.shard_map(local, mesh=mesh, in_specs=in_specs, out_specs=out_specs, check_vma=False)
```

```python
import functools
import math

import jax
import jax.numpy as jnp
from jax import lax
from jax.experimental import pallas as pl
from jax.experimental.pallas import tpu as pltpu
from jax.sharding import PartitionSpec as P

HEADS = 10
HD = 128
MASKED_SCORE = -1e30
MESH = pl.DeviceIdType.MESH
BF16 = jnp.bfloat16
F32 = jnp.float32
VMEM_BYTES = 56 * 1024 * 1024


def owner_of(head, n):
    slot, place = divmod(head, n)
    if slot and 2 * place + 2 < n:
        place = 2 * place + 2
    return place, slot


def head_in_slot(me, slot, n):
    if slot == 0:
        return me, me < HEADS
    head, valid = 0, False
    for h in range(slot * n, min(HEADS, (slot + 1) * n)):
        place = owner_of(h, n)[0]
        head = jnp.where(me == place, h, head)
        valid = jnp.logical_or(valid, me == place)
    return head, valid


def dot_nt(a, b):
    return lax.dot_general(a, b, (((1,), (1,)), ((), ())), preferred_element_type=F32)


def dot_tn(a, b):
    return lax.dot_general(a, b, (((0,), (0,)), ((), ())), preferred_element_type=F32)


def dot_nn(a, b):
    return jnp.dot(a, b, preferred_element_type=F32)


def remote(src, dst, send, recv, dp, ctx):
    return pltpu.make_async_remote_copy(
        src_ref=src, dst_ref=dst, send_sem=send, recv_sem=recv, device_id=(dp, ctx), device_id_type=MESH
    )


def greet(n, ndp):
    me, dp = lax.axis_index("ctx"), lax.axis_index("dp")
    barrier = pltpu.get_barrier_semaphore()
    for down in range(ndp):
        for step in range(n):
            if down or step:
                pl.semaphore_signal(
                    barrier, inc=1, device_id=(lax.rem(dp + down, ndp), lax.rem(me + step, n)), device_id_type=MESH
                )
    pl.semaphore_wait(barrier, n * ndp - 1)


def whole_kernel(
    n, ndp, parts, cuts, block, piece,
    seg_ref, q_ref, k_ref, v_ref, og_ref, w_hbm,
    attended_out, qg_ref, kg_ref, vg_ref, wg_out,
    heads_ref, grads_ref, attention_ref, result_ref, probs_ref, dscore_ref, turned, query_mask, key_mask,
    w_ref, og_all, att_t, att_all, grad_ref, psend_buf, precv_buf,
    xsend_buf, xrecv_buf, own_sum, chain_buf, outer_buf, middle_buf, wg_ref, att_sum,
    load_sem, send_sem, recv_sem, osend, orecv, gsend, grecv, asend, arecv, hsend, hrecv,
    psend, precv, xsend, xrecv, csend, crecv, mrecv, bsend, brecv, fsend, frecv, store_sem, wide_sem,
):
    me, dp = lax.axis_index("ctx"), lax.axis_index("dp")
    core = lax.rem(me, 2)
    chip = me // 2
    chips = n // 2
    sibling = me + 1 - 2 * core
    slots, _, seq, _ = heads_ref.shape
    rows = q_ref.shape[0]
    width = og_ref.shape[1]
    wrows = w_ref.shape[0]
    half = wrows // 2
    wide = width // parts
    broad = width // cuts
    pieces = wrows // piece
    scale = 1.0 / math.sqrt(HD)

    def record_rows(record):
        return pl.ds(pl.multiple_of(record * rows, rows), rows)

    my_rows = record_rows(me)
    loads = (
        pltpu.make_async_copy(w_hbm, w_ref, load_sem.at[0]),
        pltpu.make_async_copy(og_ref, og_all.at[record_rows(dp)], load_sem.at[1]),
    )
    for load in loads:
        load.start()
    greet(n, ndp)

    def head_columns(head):
        if isinstance(head, int):
            return pl.ds(head * HD, HD)
        return pl.ds(pl.multiple_of(head * HD, HD), HD)

    def place_of(head):
        slot = head // n
        place = head - slot * n
        if slots > 1:
            moved = 2 * place + 2
            place = jnp.where(jnp.logical_and(slot > 0, moved < n), moved, place)
        return place, slot

    def send_head(tensor, source, head, start):
        place, slot = owner_of(head, n)
        columns = head_columns(head)
        landing = heads_ref.at[slot, tensor, my_rows]
        copy = remote(
            source.at[:, columns], landing, send_sem.at[tensor, head], recv_sem.at[slot, tensor], dp, place,
        )

        @pl.when(me != place)
        def _():
            if start:
                copy.start()
            else:
                copy.wait_send()

        if start:
            @pl.when(me == place)
            def _():
                pltpu.make_async_copy(source.at[:, columns], landing, recv_sem.at[slot, tensor]).start()

    def await_head(slot, tensor):
        waited = heads_ref.at[slot, tensor]
        pltpu.make_async_copy(waited, waited, recv_sem.at[slot, tensor]).wait()

    def og_copy(source, at, count, record, slot, peer):
        landed = pl.ds(pl.multiple_of(record * rows + at, 16), count)
        return remote(source, og_all.at[landed], osend.at[slot], orecv.at[slot], peer, me)

    def send_slot(slot):
        for tensor, source in enumerate((q_ref, k_ref, v_ref)):
            for head in range(slot * n, min(HEADS, slot * n + n)):
                send_head(tensor, source, head, True)

    spread = []
    if ndp == 4:
        cut = rows // 2
        across = dp + 1 - 2 * lax.rem(dp, 2)
        along = lax.rem(dp + 2, 4)
        corner = 3 - dp
        peers = (across, along, corner)
        for order in range(2):
            for axis, peer in enumerate((across, along)):
                part = order if axis == 0 else 1 - order
                spread.append(
                    og_copy(og_ref.at[pl.ds(part * cut, cut)], part * cut, cut, dp, 2 * axis + part, peer)
                )
    else:
        peers = tuple(lax.rem(dp + ndp - step, ndp) for step in range(1, ndp))
        for step in range(1, ndp):
            spread.append(og_copy(og_ref, 0, rows, dp, step, lax.rem(dp + step, ndp)))
    for copy in spread:
        copy.start()
    send_slot(0)

    def piece_place(spot):
        feature = dp * wrows + spot * piece
        head = feature // HD
        place, slot = place_of(head)
        return place, slot, feature - head * HD

    def grad_copy(step, record, spot):
        place, slot, inside = piece_place(spot)
        return remote(
            grad_ref.at[step, pl.ds(spot * piece, piece)],
            grads_ref.at[slot, pl.ds(pl.multiple_of(inside, 16), piece), my_rows],
            gsend.at[step, spot], grecv.at[slot, inside // piece], record, place,
        )

    def make_grad(step, record):
        grad_ref[step] = dot_nt(w_ref[...], og_all[record_rows(record), :]).astype(BF16)

    def send_grad(step, record):
        for spot in range(pieces):
            if step:
                grad_copy(step, record, spot).start()
            else:
                place, slot, inside = piece_place(spot)

                @pl.when(place == me)
                def _():
                    held = pl.ds(pl.multiple_of(inside, 16), piece)
                    grads_ref[slot, held, my_rows] = grad_ref[0, pl.ds(spot * piece, piece), :]

                @pl.when(place != me)
                def _():
                    grad_copy(0, record, spot).start()

    for load in loads:
        load.wait()
    make_grad(0, dp)

    @pl.loop(0, seq // block)
    def _(index):
        at = pl.ds(pl.multiple_of(index * block, block), block)
        position = lax.broadcasted_iota(jnp.int32, (block, HD), 0) + index * block
        lane = lax.broadcasted_iota(jnp.int32, (block, HD), 1)
        count = seg_ref.shape[1]
        end = jnp.int32(0)
        segment = jnp.zeros((block, HD), jnp.int32)
        for i in range(count):
            end = end + seg_ref[0, i]
            segment = segment + jnp.where(position >= end, 1, 0)
        query_mask[at, :] = jnp.where(segment == lane, 1.0, 0.0).astype(BF16)
        key_mask[at, :] = jnp.where(jnp.logical_or(segment == lane, lane >= count), 0.0, MASKED_SCORE).astype(BF16)

    def await_og(slot, at, count, record):
        landed = og_all.at[pl.ds(pl.multiple_of(record * rows + at, 16), count)]
        remote(landed, landed, osend.at[0], orecv.at[slot], dp, me).wait_recv()
        return landed

    if ndp == 4:
        for axis, (peer, other) in enumerate(((across, along), (along, across))):
            landed = await_og(3 * axis, axis * cut, cut, peer)
            copy = og_copy(landed, axis * cut, cut, peer, 4 + axis, other)
            copy.start()
            spread.append(copy)
    for slot in range(1, slots):
        send_slot(slot)
    if ndp == 4:
        for axis, peer in enumerate((across, along)):
            await_og(axis + 1, (1 - axis) * cut, cut, peer)
            make_grad(axis + 1, peer)
    else:
        for step, peer in enumerate(peers, 1):
            await_og(step, 0, rows, peer)
            make_grad(step, peer)

    def attention_copy(slot, other, spot):
        head, _ = head_in_slot(me, slot, n)
        feature = head * HD + spot * piece
        target = feature // wrows
        row = feature - target * wrows
        landing = att_t.at[pl.ds(pl.multiple_of(row, 16), piece), record_rows(dp)]
        return target, landing, remote(
            attention_ref.at[slot, pl.ds(spot * piece, piece), record_rows(other)], landing,
            asend.at[slot, other, spot], arecv.at[dp, row // piece], target, other,
        )

    def attention_copies(slot, other, start):
        for spot in range(HD // piece):
            target, landing, copy = attention_copy(slot, other, spot)
            here = jnp.logical_and(target == dp, other == me)

            @pl.when(jnp.logical_not(here))
            def _():
                if start:
                    copy.start()
                else:
                    copy.wait_send()

            if start:
                @pl.when(here)
                def _():
                    landing[...] = attention_ref[slot, pl.ds(spot * piece, piece), my_rows]

    log2e = math.log2(math.e)

    def forward(slot):
        @pl.when(head_in_slot(me, slot, n)[1])
        def _():
            for tensor in range(3):
                await_head(slot, tensor)
            turned[...] = heads_ref[slot, 2].T

            @pl.loop(0, seq // block)
            def _(index):
                at = pl.ds(pl.multiple_of(index * block, block), block)
                left = jnp.concatenate([heads_ref[slot, 1], key_mask[...]], axis=1)
                right = jnp.concatenate([heads_ref[slot, 0, at, :], query_mask[at, :]], axis=1)
                scores = dot_nt(left, right)
                top = jnp.max(scores, axis=0, keepdims=True)
                shifted = jnp.exp2((scores - top) * (scale * log2e))
                total = jnp.sum(shifted, axis=0, keepdims=True)
                probs_b = (shifted * (1.0 / total)).astype(BF16)
                probs_ref[slot, :, at] = probs_b
                attention_ref[slot, :, at] = dot_nn(turned[...], probs_b).astype(BF16)
                for step in range(block // rows):
                    attention_copies(slot, index * (block // rows) + step, True)

    targets = (qg_ref, kg_ref, vg_ref)

    def home_copy(slot, tensor, other):
        head, _ = head_in_slot(me, slot, n)
        return remote(
            result_ref.at[slot, tensor, record_rows(other)], targets[tensor].at[:, head_columns(head)],
            hsend.at[tensor, slot, other], hrecv.at[tensor, head], dp, other,
        )

    def send_home(slot, tensor, other):
        @pl.when(other != me)
        def _():
            home_copy(slot, tensor, other).start()

        @pl.when(other == me)
        def _():
            head, _ = head_in_slot(me, slot, n)
            landing = targets[tensor].at[:, head_columns(head)]
            pltpu.make_async_copy(result_ref.at[slot, tensor, my_rows], landing, hrecv.at[tensor, head]).start()

    def receive_home(tensor):
        for head in range(HEADS):
            landed = targets[tensor].at[:, head_columns(head)]
            pltpu.make_async_copy(landed, landed, hrecv.at[tensor, head]).wait()

    def backward(slot):
        @pl.when(head_in_slot(me, slot, n)[1])
        def _():
            head, _ = head_in_slot(me, slot, n)
            turned[...] = heads_ref[slot, 1].T
            for spot in range(HD // piece):
                source = (head * HD + spot * piece) // wrows

                def await_grad(count):
                    waited = grads_ref.at[slot, pl.ds(spot * piece, piece), pl.ds(0, rows * count)]
                    pltpu.make_async_copy(waited, waited, grecv.at[slot, spot]).wait()

                pl.when(source == dp)(lambda: await_grad(n - 1))
                pl.when(source != dp)(lambda: await_grad(n))

            @pl.loop(0, seq // block)
            def _(index):
                at = pl.ds(pl.multiple_of(index * block, block), block)
                result_ref[slot, 2, at, :] = dot_nt(probs_ref[slot, at, :], grads_ref[slot]).astype(BF16)
                for step in range(block // rows):
                    send_home(slot, 2, index * (block // rows) + step)

            @pl.loop(0, seq // block)
            def _(index):
                at = pl.ds(pl.multiple_of(index * block, block), block)
                grad = grads_ref[slot, :, at]
                product = grad.astype(F32) * attention_ref[slot, :, at].astype(F32)
                grad_dot = jnp.sum(product, axis=0, keepdims=True)
                dprob = dot_nn(heads_ref[slot, 2], grad)
                dscore = (probs_ref[slot, :, at].astype(F32) * (dprob - grad_dot)).astype(BF16)
                dscore_ref[:, at] = dscore
                result_ref[slot, 0, at, :] = (dot_nn(turned[...], dscore) * scale).astype(BF16).T

            @pl.loop(0, seq // block)
            def _(index):
                at = pl.ds(pl.multiple_of(index * block, block), block)
                result_ref[slot, 1, at, :] = (dot_nn(dscore_ref[at, :], heads_ref[slot, 0]) * scale).astype(BF16)

    def send_some(slot, tensor, others):
        @pl.when(head_in_slot(me, slot, n)[1])
        def _():
            for other in others:
                send_home(slot, tensor, other)

    for slot in range(slots):
        forward(slot)
    for step, record in enumerate((dp,) + peers[:2]):
        send_grad(step, record)
    if ndp == 4:
        for axis in range(2):
            await_og(4 + axis, axis * cut, cut, corner)
        make_grad(3, corner)
    for step, record in enumerate(peers[2:], 3):
        send_grad(step, record)

    for record in range(ndp):
        for spot in range(pieces):
            landed = att_t.at[pl.ds(spot * piece, piece), pl.ds(record * rows, rows)]
            here = jnp.logical_and(record == dp, piece_place(spot)[0] == me)

            @pl.when(jnp.logical_not(here))
            def _():
                remote(landed, landed, asend.at[0, 0, 0], arecv.at[record, spot], dp, sibling).wait_recv()

    def part_columns(part):
        return pl.ds(part * wide, wide)

    def cut_columns(part):
        return pl.ds(part * broad, broad)

    my_half = pl.ds(pl.multiple_of(core * half, 16), half)
    their_half = pl.ds(pl.multiple_of((1 - core) * half, 16), half)

    def pair_copy(part):
        columns = cut_columns(part)
        return remote(
            xsend_buf.at[:, columns], xrecv_buf.at[:, columns], xsend.at[part], xrecv.at[part], dp, sibling,
        )

    def partial_copy(part, step, source, other):
        columns = cut_columns(part)
        return remote(
            psend_buf.at[record_rows(source), columns], precv_buf.at[step - 1, :, columns],
            psend.at[part, step], precv.at[part, step], other, me,
        )

    def partial_copies(part):
        if ndp == 4:
            near, far = (across, along) if 2 * part < cuts else (along, across)
            moves = ((near, near), (corner, near), (far, far))
        else:
            moves = tuple((lax.rem(dp + step, ndp),) * 2 for step in range(1, ndp))
        return tuple(functools.partial(partial_copy, part, step, *move) for step, move in enumerate(moves, 1))

    def partial_relay(part):
        far = along if 2 * part < cuts else across
        columns = cut_columns(part)
        copies = partial_copies(part)
        copies[1]().wait_recv()
        held = record_rows(far)
        total = psend_buf[held, columns].astype(F32) + precv_buf[1, :, columns].astype(F32)
        psend_buf[held, columns] = total.astype(BF16)
        copies[2]().start()

    for part in range(cuts):
        columns = cut_columns(part)
        product = dot_nn(att_t[...], og_all[:, columns])
        low, high = product[:half], product[half:]
        xsend_buf[:, columns] = jnp.where(core == 0, high, low).astype(BF16)
        own_sum[:, columns] = jnp.where(core == 0, low, high)
        pair_copy(part).start()
    att_all[...] = att_t[...].T
    order = [part for pair in zip(range(cuts // 2), range(cuts // 2, cuts)) for part in pair]
    for part in order:
        columns = cut_columns(part)
        psend_buf[:, columns] = dot_nn(att_all[...], w_ref[:, columns]).astype(BF16)
        for copy in partial_copies(part)[: 2 if ndp == 4 else ndp]:
            copy().start()
    depth = jnp.where(chip < chips // 2, chip, chips - 1 - chip)
    toward = jnp.where(chip < chips // 2, 1, -1)
    innermost = depth == chips // 2 - 1
    inner = me + 2 * toward
    outer = me - 2 * toward

    def inward_copy(part):
        columns = part_columns(part)
        return remote(
            chain_buf.at[:, columns], outer_buf.at[:, columns], csend.at[part], crecv.at[part], dp, inner,
        )

    def middle_copy(part):
        columns = part_columns(part)
        return remote(
            chain_buf.at[:, columns], middle_buf.at[:, columns], csend.at[part], mrecv.at[part], dp, inner,
        )

    def outward_copy(part):
        landed = wg_ref.at[:, part_columns(part)]
        return remote(landed, landed, bsend.at[part], brecv.at[part], dp, outer)

    def pass_copy(part, held):
        columns = part_columns(part)
        return remote(wg_ref.at[:, columns], wg_out.at[held, columns], fsend.at[part], frecv.at[part], dp, sibling)

    def wide_store(part):
        columns = part_columns(part)
        return pltpu.make_async_copy(wg_ref.at[:, columns], wg_out.at[my_half, columns], wide_sem.at[part])

    def store(part):
        columns = cut_columns(part)
        return pltpu.make_async_copy(att_sum.at[:, columns], attended_out.at[:, columns], store_sem.at[part])

    def hand_on(part):
        @pl.when(depth > 0)
        def _():
            outward_copy(part).start()

        pass_copy(part, my_half).start()
        wide_store(part).start()

    def finish_inner(part):
        columns = part_columns(part)
        middle_copy(part).wait_recv()
        total = chain_buf[:, columns].astype(F32) + middle_buf[:, columns].astype(F32)
        wg_ref[:, columns] = total.astype(BF16)
        hand_on(part)

    def chain_sum(part):
        columns = part_columns(part)
        for waited in range(cuts):
            if part * wide <= waited * broad < (part + 1) * wide:
                pair_copy(waited).wait_recv()
        own_sum[:, columns] += xrecv_buf[:, columns].astype(F32)

        @pl.when(depth > 0)
        def _():
            inward_copy(part).wait_recv()
            own_sum[:, columns] += outer_buf[:, columns].astype(F32)

        chain_buf[:, columns] = own_sum[:, columns].astype(BF16)

    @pl.when(jnp.logical_not(innermost))
    def _():
        for part in range(parts):
            chain_sum(part)
            inward_copy(part).start()

    for slot in range(slots):
        backward(slot)
        send_some(slot, 0, range(n))

    lag = 2

    @pl.when(innermost)
    def _():
        for part in range(parts):
            chain_sum(part)
            if part >= lag:
                middle_copy(part - lag).wait_send()
            middle_copy(part).start()
            if part >= lag:
                finish_inner(part - lag)
            for slot in range(slots):
                send_some(slot, 1, range(part * n // parts, (part + 1) * n // parts))
            if ndp == 4 and part >= parts - cuts:
                partial_relay(order[part - parts + cuts])
        for part in range(parts - lag, parts):
            finish_inner(part)

    @pl.when(jnp.logical_not(innermost))
    def _():
        for slot in range(slots):
            send_some(slot, 1, range(n))
        if ndp == 4:
            for part in order:
                partial_relay(part)

    for part in order:
        columns = cut_columns(part)
        total = psend_buf[record_rows(dp), columns].astype(F32)
        for step, copy in enumerate(partial_copies(part)):
            if ndp != 4 or step != 1:
                copy().wait_recv()
                total = total + precv_buf[step, :, columns].astype(F32)
        att_sum[:, columns] = total.astype(BF16)
        store(part).start()

    for part in range(parts):
        @pl.when(jnp.logical_not(innermost))
        def _():
            outward_copy(part).wait_recv()
            hand_on(part)

    for tensor in range(3):
        receive_home(tensor)
    for part in range(parts):
        pass_copy(part, their_half).wait_recv()

    for tensor, source in enumerate((q_ref, k_ref, v_ref)):
        for head in range(HEADS):
            send_head(tensor, source, head, False)
    for copy in spread:
        copy.wait_send()
    for step, record in enumerate((dp,) + peers):
        for spot in range(pieces):
            copy = grad_copy(step, record, spot)
            if step:
                copy.wait_send()
            else:
                pl.when(piece_place(spot)[0] != me)(copy.wait_send)
    for slot in range(slots):
        @pl.when(head_in_slot(me, slot, n)[1])
        def _():
            for other in range(n):
                attention_copies(slot, other, False)
                for tensor in range(3):
                    pl.when(other != me)(home_copy(slot, tensor, other).wait_send)
    for part in range(cuts):
        pair_copy(part).wait_send()
        for copy in partial_copies(part):
            copy().wait_send()
    for part in range(parts):
        if part >= parts - lag:
            inward_copy(part).wait_send()
        else:
            pl.when(jnp.logical_not(innermost))(inward_copy(part).wait_send)
        pl.when(depth > 0)(outward_copy(part).wait_send)
        pass_copy(part, my_half).wait_send()
        wide_store(part).wait()
    for part in range(cuts):
        store(part).wait()


def copy_kernel(pieces, *refs):
    sources, targets, held = refs[:5], refs[5:10], refs[10:15]
    wide_held, in_sem, out_sem = refs[15:]
    spans = []
    for i in (4, 0, 1, 2, 3):
        rows = held[i].shape[0] // (pieces if i == 4 else 2)
        spans += [(i, pl.ds(at, rows)) for at in range(0, held[i].shape[0], rows)]
    loads = [pltpu.make_async_copy(sources[i].at[x], held[i].at[x], in_sem.at[j]) for j, (i, x) in enumerate(spans)]
    stores = [
        pltpu.make_async_copy((held[i] if i < 4 else wide_held).at[x], targets[i].at[x], out_sem.at[j])
        for j, (i, x) in enumerate(spans)
    ]
    for load in loads:
        load.start()
    for j, (i, x) in enumerate(spans):
        loads[j].wait()
        if i == 4:
            wide_held[x, :] = held[4][x, :].astype(F32)
        stores[j].start()
    for store in stores:
        store.wait()


def local(queries, keys, values, seg_lengths, out_grad, w_out):
    n, ndp = lax.axis_size("ctx"), lax.axis_size("dp")
    rows, inner = queries.shape[1:]
    width = out_grad.shape[2]
    seq = rows * n
    wrows = w_out.shape[0]
    half = wrows // 2
    slots = -(-HEADS // n)
    parts, cuts = 10, 4
    block = math.gcd(512, seq)
    piece = math.gcd(HD, wrows)
    shape = jax.ShapeDtypeStruct
    dma = pltpu.SemaphoreType.DMA
    out_shape = (
        shape((rows, width), BF16), shape((rows, inner), BF16), shape((rows, inner), BF16),
        shape((rows, inner), BF16), shape((wrows, width), F32),
    )
    anywhere = [pl.BlockSpec(memory_space=pl.ANY)] * 5
    outputs = pl.pallas_call(
        functools.partial(whole_kernel, n, ndp, parts, cuts, block, piece),
        out_shape=out_shape[:4] + (shape((wrows, width), BF16),),
        in_specs=[pl.BlockSpec(memory_space=pltpu.SMEM)] + anywhere,
        out_specs=tuple(anywhere),
        scratch_shapes=[
            pltpu.VMEM((slots, 3, seq, HD), BF16),
            pltpu.VMEM((slots, HD, seq), BF16),
            pltpu.VMEM((slots, HD, seq), BF16),
            pltpu.VMEM((slots, 3, seq, HD), BF16),
            pltpu.VMEM((slots, seq, seq), BF16),
            pltpu.VMEM((seq, seq), BF16),
            pltpu.VMEM((HD, seq), BF16),
            pltpu.VMEM((seq, HD), BF16),
            pltpu.VMEM((seq, HD), BF16),
            pltpu.VMEM((wrows, width), BF16),
            pltpu.VMEM((ndp * rows, width), BF16),
            pltpu.VMEM((wrows, ndp * rows), BF16),
            pltpu.VMEM((ndp * rows, wrows), BF16),
            pltpu.VMEM((ndp, wrows, rows), BF16),
            pltpu.VMEM((ndp * rows, width), BF16),
            pltpu.VMEM((ndp - 1, rows, width), BF16),
            pltpu.VMEM((half, width), BF16),
            pltpu.VMEM((half, width), BF16),
            pltpu.VMEM((half, width), F32),
            pltpu.VMEM((half, width), BF16),
            pltpu.VMEM((half, width), BF16),
            pltpu.VMEM((half, width), BF16),
            pltpu.VMEM((half, width), BF16),
            pltpu.VMEM((rows, width), BF16),
            dma((2,)), dma((3, HEADS)), dma((slots, 3)), dma((max(ndp, 6),)), dma((max(ndp, 6),)),
            dma((ndp, wrows // piece)), dma((slots, HD // piece)), dma((slots, n, HD // piece)), dma((ndp, wrows // piece)),
            dma((3, slots, n)), dma((3, HEADS)),
            dma((cuts, ndp)), dma((cuts, ndp)), dma((cuts,)), dma((cuts,)),
            dma((parts,)), dma((parts,)), dma((parts,)), dma((parts,)), dma((parts,)), dma((parts,)), dma((parts,)),
            dma((cuts,)), dma((parts,)),
        ],
        compiler_params=pltpu.CompilerParams(
            collective_id=0, has_side_effects=True, vmem_limit_bytes=VMEM_BYTES
        ),
    )(seg_lengths, queries[0], keys[0], values[0], out_grad[0], w_out)
    attended, query_grad, key_grad, value_grad, weight_grad = pl.pallas_call(
        functools.partial(copy_kernel, 5),
        out_shape=out_shape,
        in_specs=anywhere,
        out_specs=tuple(anywhere),
        scratch_shapes=[pltpu.VMEM(x.shape, BF16) for x in out_shape]
        + [pltpu.VMEM((wrows, width), F32), dma((13,)), dma((13,))],
        compiler_params=pltpu.CompilerParams(vmem_limit_bytes=VMEM_BYTES),
    )(*outputs)
    return (attended[None], query_grad[None], key_grad[None], value_grad[None], weight_grad)


def solution(mesh):
    in_specs = (
        P("dp", "ctx", None),
        P("dp", "ctx", None),
        P("dp", "ctx", None),
        P("dp", None),
        P("dp", "ctx", None),
        P("dp", None),
    )
    out_specs = (
        P("dp", "ctx", None),
        P("dp", "ctx", None),
        P("dp", "ctx", None),
        P("dp", "ctx", None),
        P("dp", None),
    )
    return jax.shard_map(local, mesh=mesh, in_specs=in_specs, out_specs=out_specs, check_vma=False)
```

```python
import functools
import math

import jax
import jax.numpy as jnp
from jax import lax
from jax.experimental import pallas as pl
from jax.experimental.pallas import tpu as pltpu
from jax.sharding import PartitionSpec as P

HEADS = 10
HD = 128
MASKED_SCORE = -1e30
MESH = pl.DeviceIdType.MESH
BF16 = jnp.bfloat16
F32 = jnp.float32
VMEM_BYTES = 56 * 1024 * 1024


def owner_of(head, n):
    slot, place = divmod(head, n)
    if slot and 2 * place + 2 < n:
        place = 2 * place + 2
    return place, slot


def head_in_slot(me, slot, n):
    if slot == 0:
        return me, me < HEADS
    head, valid = 0, False
    for h in range(slot * n, min(HEADS, (slot + 1) * n)):
        place = owner_of(h, n)[0]
        head = jnp.where(me == place, h, head)
        valid = jnp.logical_or(valid, me == place)
    return head, valid


def dot_nt(a, b):
    return lax.dot_general(a, b, (((1,), (1,)), ((), ())), preferred_element_type=F32)


def dot_tn(a, b):
    return lax.dot_general(a, b, (((0,), (0,)), ((), ())), preferred_element_type=F32)


def dot_nn(a, b):
    return jnp.dot(a, b, preferred_element_type=F32)


def remote(src, dst, send, recv, dp, ctx):
    return pltpu.make_async_remote_copy(
        src_ref=src, dst_ref=dst, send_sem=send, recv_sem=recv, device_id=(dp, ctx), device_id_type=MESH
    )


def greet(n, ndp):
    me, dp = lax.axis_index("ctx"), lax.axis_index("dp")
    barrier = pltpu.get_barrier_semaphore()
    for down in range(ndp):
        for step in range(n):
            if down or step:
                pl.semaphore_signal(
                    barrier, inc=1, device_id=(lax.rem(dp + down, ndp), lax.rem(me + step, n)), device_id_type=MESH
                )
    pl.semaphore_wait(barrier, n * ndp - 1)


def whole_kernel(
    n, ndp, parts, cuts, block, piece,
    seg_ref, q_ref, k_ref, v_ref, og_ref, w_hbm,
    attended_out, qg_ref, kg_ref, vg_ref, wg_out,
    heads_ref, grads_ref, attention_ref, result_ref, probs_ref, dscore_ref, turned, query_mask, key_mask,
    w_ref, og_all, att_t, att_all, grad_ref, psend_buf, precv_buf,
    xsend_buf, xrecv_buf, own_sum, chain_buf, outer_buf, middle_buf, wg_ref, att_sum,
    load_sem, send_sem, recv_sem, osend, orecv, gsend, grecv, asend, arecv, hsend, hrecv,
    psend, precv, xsend, xrecv, csend, crecv, mrecv, bsend, brecv, fsend, frecv, store_sem, wide_sem,
):
    me, dp = lax.axis_index("ctx"), lax.axis_index("dp")
    core = lax.rem(me, 2)
    chip = me // 2
    chips = n // 2
    sibling = me + 1 - 2 * core
    slots, _, seq, _ = heads_ref.shape
    rows = q_ref.shape[0]
    width = og_ref.shape[1]
    wrows = w_ref.shape[0]
    half = wrows // 2
    wide = width // parts
    broad = width // cuts
    pieces = wrows // piece
    scale = 1.0 / math.sqrt(HD)

    def record_rows(record):
        return pl.ds(pl.multiple_of(record * rows, rows), rows)

    my_rows = record_rows(me)
    loads = (
        pltpu.make_async_copy(w_hbm, w_ref, load_sem.at[0]),
        pltpu.make_async_copy(og_ref, og_all.at[record_rows(dp)], load_sem.at[1]),
    )
    for load in loads:
        load.start()
    greet(n, ndp)

    def head_columns(head):
        if isinstance(head, int):
            return pl.ds(head * HD, HD)
        return pl.ds(pl.multiple_of(head * HD, HD), HD)

    def place_of(head):
        slot = head // n
        place = head - slot * n
        if slots > 1:
            moved = 2 * place + 2
            place = jnp.where(jnp.logical_and(slot > 0, moved < n), moved, place)
        return place, slot

    def send_head(tensor, source, head, start):
        place, slot = owner_of(head, n)
        columns = head_columns(head)
        landing = heads_ref.at[slot, tensor, my_rows]
        copy = remote(
            source.at[:, columns], landing, send_sem.at[tensor, head], recv_sem.at[slot, tensor], dp, place,
        )

        @pl.when(me != place)
        def _():
            if start:
                copy.start()
            else:
                copy.wait_send()

        if start:
            @pl.when(me == place)
            def _():
                pltpu.make_async_copy(source.at[:, columns], landing, recv_sem.at[slot, tensor]).start()

    def await_head(slot, tensor):
        waited = heads_ref.at[slot, tensor]
        pltpu.make_async_copy(waited, waited, recv_sem.at[slot, tensor]).wait()

    def og_copy(source, at, count, record, slot, peer):
        landed = pl.ds(pl.multiple_of(record * rows + at, 16), count)
        return remote(source, og_all.at[landed], osend.at[slot], orecv.at[slot], peer, me)

    def send_slot(slot):
        for tensor, source in enumerate((q_ref, k_ref, v_ref)):
            for head in range(slot * n, min(HEADS, slot * n + n)):
                send_head(tensor, source, head, True)

    spread = []
    if ndp == 4:
        cut = rows // 2
        across = dp + 1 - 2 * lax.rem(dp, 2)
        along = lax.rem(dp + 2, 4)
        corner = 3 - dp
        peers = (across, along, corner)
        for order in range(2):
            for axis, peer in enumerate((across, along)):
                part = order if axis == 0 else 1 - order
                spread.append(
                    og_copy(og_ref.at[pl.ds(part * cut, cut)], part * cut, cut, dp, 2 * axis + part, peer)
                )
    else:
        peers = tuple(lax.rem(dp + ndp - step, ndp) for step in range(1, ndp))
        for step in range(1, ndp):
            spread.append(og_copy(og_ref, 0, rows, dp, step, lax.rem(dp + step, ndp)))
    for copy in spread:
        copy.start()
    send_slot(0)

    def piece_place(spot):
        feature = dp * wrows + spot * piece
        head = feature // HD
        place, slot = place_of(head)
        return place, slot, feature - head * HD

    def grad_copy(step, record, spot):
        place, slot, inside = piece_place(spot)
        return remote(
            grad_ref.at[step, pl.ds(spot * piece, piece)],
            grads_ref.at[slot, pl.ds(pl.multiple_of(inside, 16), piece), my_rows],
            gsend.at[step, spot], grecv.at[slot, inside // piece], record, place,
        )

    def make_grad(step, record):
        grad_ref[step] = dot_nt(w_ref[...], og_all[record_rows(record), :]).astype(BF16)

    def send_grad(step, record):
        for spot in range(pieces):
            if step:
                grad_copy(step, record, spot).start()
            else:
                place, slot, inside = piece_place(spot)

                @pl.when(place == me)
                def _():
                    held = pl.ds(pl.multiple_of(inside, 16), piece)
                    grads_ref[slot, held, my_rows] = grad_ref[0, pl.ds(spot * piece, piece), :]

                @pl.when(place != me)
                def _():
                    grad_copy(0, record, spot).start()

    for load in loads:
        load.wait()
    make_grad(0, dp)

    @pl.loop(0, seq // block)
    def _(index):
        at = pl.ds(pl.multiple_of(index * block, block), block)
        position = lax.broadcasted_iota(jnp.int32, (block, HD), 0) + index * block
        lane = lax.broadcasted_iota(jnp.int32, (block, HD), 1)
        count = seg_ref.shape[1]
        end = jnp.int32(0)
        segment = jnp.zeros((block, HD), jnp.int32)
        for i in range(count):
            end = end + seg_ref[0, i]
            segment = segment + jnp.where(position >= end, 1, 0)
        query_mask[at, :] = jnp.where(segment == lane, 1.0, 0.0).astype(BF16)
        key_mask[at, :] = jnp.where(jnp.logical_or(segment == lane, lane >= count), 0.0, MASKED_SCORE).astype(BF16)

    def await_og(slot, at, count, record):
        landed = og_all.at[pl.ds(pl.multiple_of(record * rows + at, 16), count)]
        remote(landed, landed, osend.at[0], orecv.at[slot], dp, me).wait_recv()
        return landed

    if ndp == 4:
        for axis, (peer, other) in enumerate(((across, along), (along, across))):
            landed = await_og(3 * axis, axis * cut, cut, peer)
            copy = og_copy(landed, axis * cut, cut, peer, 4 + axis, other)
            copy.start()
            spread.append(copy)
    for slot in range(1, slots):
        send_slot(slot)
    if ndp == 4:
        for axis, peer in enumerate((across, along)):
            await_og(axis + 1, (1 - axis) * cut, cut, peer)
            make_grad(axis + 1, peer)
    else:
        for step, peer in enumerate(peers, 1):
            await_og(step, 0, rows, peer)
            make_grad(step, peer)

    def attention_copy(slot, other, spot):
        head, _ = head_in_slot(me, slot, n)
        feature = head * HD + spot * piece
        target = feature // wrows
        row = feature - target * wrows
        landing = att_t.at[pl.ds(pl.multiple_of(row, 16), piece), record_rows(dp)]
        return target, landing, remote(
            attention_ref.at[slot, pl.ds(spot * piece, piece), record_rows(other)], landing,
            asend.at[slot, other, spot], arecv.at[dp, row // piece], target, other,
        )

    def attention_copies(slot, other, start):
        for spot in range(HD // piece):
            target, landing, copy = attention_copy(slot, other, spot)
            here = jnp.logical_and(target == dp, other == me)

            @pl.when(jnp.logical_not(here))
            def _():
                if start:
                    copy.start()
                else:
                    copy.wait_send()

            if start:
                @pl.when(here)
                def _():
                    landing[...] = attention_ref[slot, pl.ds(spot * piece, piece), my_rows]

    log2e = math.log2(math.e)

    def forward(slot):
        @pl.when(head_in_slot(me, slot, n)[1])
        def _():
            for tensor in range(3):
                await_head(slot, tensor)
            turned[...] = heads_ref[slot, 2].T

            @pl.loop(0, seq // block)
            def _(index):
                at = pl.ds(pl.multiple_of(index * block, block), block)
                left = jnp.concatenate([heads_ref[slot, 1], key_mask[...]], axis=1)
                right = jnp.concatenate([heads_ref[slot, 0, at, :], query_mask[at, :]], axis=1)
                scores = dot_nt(left, right)
                top = jnp.max(scores, axis=0, keepdims=True)
                shifted = jnp.exp2((scores - top) * (scale * log2e))
                total = jnp.sum(shifted, axis=0, keepdims=True)
                probs_b = (shifted * (1.0 / total)).astype(BF16)
                probs_ref[slot, :, at] = probs_b
                attention_ref[slot, :, at] = dot_nn(turned[...], probs_b).astype(BF16)
                for step in range(block // rows):
                    attention_copies(slot, index * (block // rows) + step, True)

    targets = (qg_ref, kg_ref, vg_ref)

    def home_copy(slot, tensor, other):
        head, _ = head_in_slot(me, slot, n)
        return remote(
            result_ref.at[slot, tensor, record_rows(other)], targets[tensor].at[:, head_columns(head)],
            hsend.at[tensor, slot, other], hrecv.at[tensor, head], dp, other,
        )

    def send_home(slot, tensor, other):
        @pl.when(other != me)
        def _():
            home_copy(slot, tensor, other).start()

        @pl.when(other == me)
        def _():
            head, _ = head_in_slot(me, slot, n)
            landing = targets[tensor].at[:, head_columns(head)]
            pltpu.make_async_copy(result_ref.at[slot, tensor, my_rows], landing, hrecv.at[tensor, head]).start()

    def receive_home(tensor):
        for head in range(HEADS):
            landed = targets[tensor].at[:, head_columns(head)]
            pltpu.make_async_copy(landed, landed, hrecv.at[tensor, head]).wait()

    def backward(slot):
        @pl.when(head_in_slot(me, slot, n)[1])
        def _():
            head, _ = head_in_slot(me, slot, n)
            turned[...] = heads_ref[slot, 1].T
            for spot in range(HD // piece):
                source = (head * HD + spot * piece) // wrows

                def await_grad(count):
                    waited = grads_ref.at[slot, pl.ds(spot * piece, piece), pl.ds(0, rows * count)]
                    pltpu.make_async_copy(waited, waited, grecv.at[slot, spot]).wait()

                pl.when(source == dp)(lambda: await_grad(n - 1))
                pl.when(source != dp)(lambda: await_grad(n))

            @pl.loop(0, seq // block)
            def _(index):
                at = pl.ds(pl.multiple_of(index * block, block), block)
                result_ref[slot, 2, at, :] = dot_nt(probs_ref[slot, at, :], grads_ref[slot]).astype(BF16)
                for step in range(block // rows):
                    send_home(slot, 2, index * (block // rows) + step)

            @pl.loop(0, seq // block)
            def _(index):
                at = pl.ds(pl.multiple_of(index * block, block), block)
                grad = grads_ref[slot, :, at]
                product = grad.astype(F32) * attention_ref[slot, :, at].astype(F32)
                grad_dot = jnp.sum(product, axis=0, keepdims=True)
                dprob = dot_nn(heads_ref[slot, 2], grad)
                dscore = (probs_ref[slot, :, at].astype(F32) * (dprob - grad_dot)).astype(BF16)
                dscore_ref[:, at] = dscore
                result_ref[slot, 0, at, :] = (dot_nn(turned[...], dscore) * scale).astype(BF16).T

            @pl.loop(0, seq // block)
            def _(index):
                at = pl.ds(pl.multiple_of(index * block, block), block)
                result_ref[slot, 1, at, :] = (dot_nn(dscore_ref[at, :], heads_ref[slot, 0]) * scale).astype(BF16)

    def send_some(slot, tensor, others):
        @pl.when(head_in_slot(me, slot, n)[1])
        def _():
            for other in others:
                send_home(slot, tensor, other)

    for slot in range(slots):
        forward(slot)
    for step, record in enumerate((dp,) + peers[:2]):
        send_grad(step, record)
    if ndp == 4:
        for axis in range(2):
            await_og(4 + axis, axis * cut, cut, corner)
        make_grad(3, corner)
    for step, record in enumerate(peers[2:], 3):
        send_grad(step, record)

    for record in range(ndp):
        for spot in range(pieces):
            landed = att_t.at[pl.ds(spot * piece, piece), pl.ds(record * rows, rows)]
            here = jnp.logical_and(record == dp, piece_place(spot)[0] == me)

            @pl.when(jnp.logical_not(here))
            def _():
                remote(landed, landed, asend.at[0, 0, 0], arecv.at[record, spot], dp, sibling).wait_recv()

    def part_columns(part):
        return pl.ds(part * wide, wide)

    def cut_columns(part):
        return pl.ds(part * broad, broad)

    my_half = pl.ds(pl.multiple_of(core * half, 16), half)
    their_half = pl.ds(pl.multiple_of((1 - core) * half, 16), half)

    def pair_copy(part):
        columns = cut_columns(part)
        return remote(
            xsend_buf.at[:, columns], xrecv_buf.at[:, columns], xsend.at[part], xrecv.at[part], dp, sibling,
        )

    def partial_copy(part, step, source, other):
        columns = cut_columns(part)
        return remote(
            psend_buf.at[record_rows(source), columns], precv_buf.at[step - 1, :, columns],
            psend.at[part, step], precv.at[part, step], other, me,
        )

    def partial_copies(part):
        if ndp == 4:
            near, far = (across, along) if 2 * part < cuts else (along, across)
            moves = ((near, near), (corner, near), (far, far))
        else:
            moves = tuple((lax.rem(dp + step, ndp),) * 2 for step in range(1, ndp))
        return tuple(functools.partial(partial_copy, part, step, *move) for step, move in enumerate(moves, 1))

    def partial_relay(part):
        far = along if 2 * part < cuts else across
        columns = cut_columns(part)
        copies = partial_copies(part)
        copies[1]().wait_recv()
        held = record_rows(far)
        total = psend_buf[held, columns].astype(F32) + precv_buf[1, :, columns].astype(F32)
        psend_buf[held, columns] = total.astype(BF16)
        copies[2]().start()

    for part in range(cuts):
        columns = cut_columns(part)
        product = dot_nn(att_t[...], og_all[:, columns])
        low, high = product[:half], product[half:]
        xsend_buf[:, columns] = jnp.where(core == 0, high, low).astype(BF16)
        own_sum[:, columns] = jnp.where(core == 0, low, high)
        pair_copy(part).start()
    att_all[...] = att_t[...].T
    order = [part for pair in zip(range(cuts // 2), range(cuts // 2, cuts)) for part in pair]
    for part in order:
        columns = cut_columns(part)
        psend_buf[:, columns] = dot_nn(att_all[...], w_ref[:, columns]).astype(BF16)
        for copy in partial_copies(part)[: 2 if ndp == 4 else ndp]:
            copy().start()
    depth = jnp.where(chip < chips // 2, chip, chips - 1 - chip)
    toward = jnp.where(chip < chips // 2, 1, -1)
    innermost = depth == chips // 2 - 1
    inner = me + 2 * toward
    outer = me - 2 * toward

    def inward_copy(part):
        columns = part_columns(part)
        return remote(
            chain_buf.at[:, columns], outer_buf.at[:, columns], csend.at[part], crecv.at[part], dp, inner,
        )

    def middle_copy(part):
        columns = part_columns(part)
        return remote(
            chain_buf.at[:, columns], middle_buf.at[:, columns], csend.at[part], mrecv.at[part], dp, inner,
        )

    def outward_copy(part):
        landed = wg_ref.at[:, part_columns(part)]
        return remote(landed, landed, bsend.at[part], brecv.at[part], dp, outer)

    def pass_copy(part, held):
        columns = part_columns(part)
        return remote(wg_ref.at[:, columns], wg_out.at[held, columns], fsend.at[part], frecv.at[part], dp, sibling)

    def wide_store(part):
        columns = part_columns(part)
        return pltpu.make_async_copy(wg_ref.at[:, columns], wg_out.at[my_half, columns], wide_sem.at[part])

    def store(part):
        columns = cut_columns(part)
        return pltpu.make_async_copy(att_sum.at[:, columns], attended_out.at[:, columns], store_sem.at[part])

    def hand_on(part):
        @pl.when(depth > 0)
        def _():
            outward_copy(part).start()

        pass_copy(part, my_half).start()
        wide_store(part).start()

    def finish_inner(part):
        columns = part_columns(part)
        middle_copy(part).wait_recv()
        total = chain_buf[:, columns].astype(F32) + middle_buf[:, columns].astype(F32)
        wg_ref[:, columns] = total.astype(BF16)
        hand_on(part)

    def chain_sum(part):
        columns = part_columns(part)
        for waited in range(cuts):
            if part * wide <= waited * broad < (part + 1) * wide:
                pair_copy(waited).wait_recv()
        own_sum[:, columns] += xrecv_buf[:, columns].astype(F32)

        @pl.when(depth > 0)
        def _():
            inward_copy(part).wait_recv()
            own_sum[:, columns] += outer_buf[:, columns].astype(F32)

        chain_buf[:, columns] = own_sum[:, columns].astype(BF16)

    @pl.when(jnp.logical_not(innermost))
    def _():
        for part in range(parts):
            chain_sum(part)
            inward_copy(part).start()

    for slot in range(slots):
        backward(slot)
        send_some(slot, 0, range(n))

    lag = 4

    @pl.when(innermost)
    def _():
        for part in range(parts):
            chain_sum(part)
            if part >= lag:
                middle_copy(part - lag).wait_send()
            middle_copy(part).start()
            if part >= lag:
                finish_inner(part - lag)
            for slot in range(slots):
                send_some(slot, 1, range(part * n // parts, (part + 1) * n // parts))
            if ndp == 4 and part >= parts - cuts:
                partial_relay(order[part - parts + cuts])
        for part in range(parts - lag, parts):
            finish_inner(part)

    @pl.when(jnp.logical_not(innermost))
    def _():
        for slot in range(slots):
            send_some(slot, 1, range(n))
        if ndp == 4:
            for part in order:
                partial_relay(part)

    for part in order:
        columns = cut_columns(part)
        total = psend_buf[record_rows(dp), columns].astype(F32)
        for step, copy in enumerate(partial_copies(part)):
            if ndp != 4 or step != 1:
                copy().wait_recv()
                total = total + precv_buf[step, :, columns].astype(F32)
        att_sum[:, columns] = total.astype(BF16)
        store(part).start()

    for part in range(parts):
        @pl.when(jnp.logical_not(innermost))
        def _():
            outward_copy(part).wait_recv()
            hand_on(part)

    for tensor in range(3):
        receive_home(tensor)
    for part in range(parts):
        pass_copy(part, their_half).wait_recv()

    for tensor, source in enumerate((q_ref, k_ref, v_ref)):
        for head in range(HEADS):
            send_head(tensor, source, head, False)
    for copy in spread:
        copy.wait_send()
    for step, record in enumerate((dp,) + peers):
        for spot in range(pieces):
            copy = grad_copy(step, record, spot)
            if step:
                copy.wait_send()
            else:
                pl.when(piece_place(spot)[0] != me)(copy.wait_send)
    for slot in range(slots):
        @pl.when(head_in_slot(me, slot, n)[1])
        def _():
            for other in range(n):
                attention_copies(slot, other, False)
                for tensor in range(3):
                    pl.when(other != me)(home_copy(slot, tensor, other).wait_send)
    for part in range(cuts):
        pair_copy(part).wait_send()
        for copy in partial_copies(part):
            copy().wait_send()
    for part in range(parts):
        if part >= parts - lag:
            inward_copy(part).wait_send()
        else:
            pl.when(jnp.logical_not(innermost))(inward_copy(part).wait_send)
        pl.when(depth > 0)(outward_copy(part).wait_send)
        pass_copy(part, my_half).wait_send()
        wide_store(part).wait()
    for part in range(cuts):
        store(part).wait()


def copy_kernel(pieces, *refs):
    sources, targets, held = refs[:5], refs[5:10], refs[10:15]
    wide_held, in_sem, out_sem = refs[15:]
    spans = []
    for i in (4, 0, 1, 2, 3):
        rows = held[i].shape[0] // (pieces if i == 4 else 2)
        spans += [(i, pl.ds(at, rows)) for at in range(0, held[i].shape[0], rows)]
    loads = [pltpu.make_async_copy(sources[i].at[x], held[i].at[x], in_sem.at[j]) for j, (i, x) in enumerate(spans)]
    stores = [
        pltpu.make_async_copy((held[i] if i < 4 else wide_held).at[x], targets[i].at[x], out_sem.at[j])
        for j, (i, x) in enumerate(spans)
    ]
    for load in loads:
        load.start()
    for j, (i, x) in enumerate(spans):
        loads[j].wait()
        if i == 4:
            wide_held[x, :] = held[4][x, :].astype(F32)
        stores[j].start()
    for store in stores:
        store.wait()


def local(queries, keys, values, seg_lengths, out_grad, w_out):
    n, ndp = lax.axis_size("ctx"), lax.axis_size("dp")
    rows, inner = queries.shape[1:]
    width = out_grad.shape[2]
    seq = rows * n
    wrows = w_out.shape[0]
    half = wrows // 2
    slots = -(-HEADS // n)
    parts, cuts = 10, 4
    block = math.gcd(512, seq)
    piece = math.gcd(HD, wrows)
    shape = jax.ShapeDtypeStruct
    dma = pltpu.SemaphoreType.DMA
    out_shape = (
        shape((rows, width), BF16), shape((rows, inner), BF16), shape((rows, inner), BF16),
        shape((rows, inner), BF16), shape((wrows, width), F32),
    )
    anywhere = [pl.BlockSpec(memory_space=pl.ANY)] * 5
    outputs = pl.pallas_call(
        functools.partial(whole_kernel, n, ndp, parts, cuts, block, piece),
        out_shape=out_shape[:4] + (shape((wrows, width), BF16),),
        in_specs=[pl.BlockSpec(memory_space=pltpu.SMEM)] + anywhere,
        out_specs=tuple(anywhere),
        scratch_shapes=[
            pltpu.VMEM((slots, 3, seq, HD), BF16),
            pltpu.VMEM((slots, HD, seq), BF16),
            pltpu.VMEM((slots, HD, seq), BF16),
            pltpu.VMEM((slots, 3, seq, HD), BF16),
            pltpu.VMEM((slots, seq, seq), BF16),
            pltpu.VMEM((seq, seq), BF16),
            pltpu.VMEM((HD, seq), BF16),
            pltpu.VMEM((seq, HD), BF16),
            pltpu.VMEM((seq, HD), BF16),
            pltpu.VMEM((wrows, width), BF16),
            pltpu.VMEM((ndp * rows, width), BF16),
            pltpu.VMEM((wrows, ndp * rows), BF16),
            pltpu.VMEM((ndp * rows, wrows), BF16),
            pltpu.VMEM((ndp, wrows, rows), BF16),
            pltpu.VMEM((ndp * rows, width), BF16),
            pltpu.VMEM((ndp - 1, rows, width), BF16),
            pltpu.VMEM((half, width), BF16),
            pltpu.VMEM((half, width), BF16),
            pltpu.VMEM((half, width), F32),
            pltpu.VMEM((half, width), BF16),
            pltpu.VMEM((half, width), BF16),
            pltpu.VMEM((half, width), BF16),
            pltpu.VMEM((half, width), BF16),
            pltpu.VMEM((rows, width), BF16),
            dma((2,)), dma((3, HEADS)), dma((slots, 3)), dma((max(ndp, 6),)), dma((max(ndp, 6),)),
            dma((ndp, wrows // piece)), dma((slots, HD // piece)), dma((slots, n, HD // piece)), dma((ndp, wrows // piece)),
            dma((3, slots, n)), dma((3, HEADS)),
            dma((cuts, ndp)), dma((cuts, ndp)), dma((cuts,)), dma((cuts,)),
            dma((parts,)), dma((parts,)), dma((parts,)), dma((parts,)), dma((parts,)), dma((parts,)), dma((parts,)),
            dma((cuts,)), dma((parts,)),
        ],
        compiler_params=pltpu.CompilerParams(
            collective_id=0, has_side_effects=True, vmem_limit_bytes=VMEM_BYTES
        ),
    )(seg_lengths, queries[0], keys[0], values[0], out_grad[0], w_out)
    attended, query_grad, key_grad, value_grad, weight_grad = pl.pallas_call(
        functools.partial(copy_kernel, 5),
        out_shape=out_shape,
        in_specs=anywhere,
        out_specs=tuple(anywhere),
        scratch_shapes=[pltpu.VMEM(x.shape, BF16) for x in out_shape]
        + [pltpu.VMEM((wrows, width), F32), dma((13,)), dma((13,))],
        compiler_params=pltpu.CompilerParams(vmem_limit_bytes=VMEM_BYTES),
    )(*outputs)
    return (attended[None], query_grad[None], key_grad[None], value_grad[None], weight_grad)


def solution(mesh):
    in_specs = (
        P("dp", "ctx", None),
        P("dp", "ctx", None),
        P("dp", "ctx", None),
        P("dp", None),
        P("dp", "ctx", None),
        P("dp", None),
    )
    out_specs = (
        P("dp", "ctx", None),
        P("dp", "ctx", None),
        P("dp", "ctx", None),
        P("dp", "ctx", None),
        P("dp", None),
    )
    return jax.shard_map(local, mesh=mesh, in_specs=in_specs, out_specs=out_specs, check_vma=False)
```

```python
import functools
import math

import jax
import jax.numpy as jnp
from jax import lax
from jax.experimental import pallas as pl
from jax.experimental.pallas import tpu as pltpu
from jax.sharding import PartitionSpec as P

HEADS = 10
HD = 128
MASKED_SCORE = -1e30
MESH = pl.DeviceIdType.MESH
BF16 = jnp.bfloat16
F32 = jnp.float32
VMEM_BYTES = 56 * 1024 * 1024


def owner_of(head, n):
    slot, place = divmod(head, n)
    if slot and 2 * place + 2 < n:
        place = 2 * place + 2
    return place, slot


def head_in_slot(me, slot, n):
    if slot == 0:
        return me, me < HEADS
    head, valid = 0, False
    for h in range(slot * n, min(HEADS, (slot + 1) * n)):
        place = owner_of(h, n)[0]
        head = jnp.where(me == place, h, head)
        valid = jnp.logical_or(valid, me == place)
    return head, valid


def dot_nt(a, b):
    return lax.dot_general(a, b, (((1,), (1,)), ((), ())), preferred_element_type=F32)


def dot_tn(a, b):
    return lax.dot_general(a, b, (((0,), (0,)), ((), ())), preferred_element_type=F32)


def dot_nn(a, b):
    return jnp.dot(a, b, preferred_element_type=F32)


def remote(src, dst, send, recv, dp, ctx):
    return pltpu.make_async_remote_copy(
        src_ref=src, dst_ref=dst, send_sem=send, recv_sem=recv, device_id=(dp, ctx), device_id_type=MESH
    )


def greet(n, ndp):
    me, dp = lax.axis_index("ctx"), lax.axis_index("dp")
    barrier = pltpu.get_barrier_semaphore()
    for down in range(ndp):
        for step in range(n):
            if down or step:
                pl.semaphore_signal(
                    barrier, inc=1, device_id=(lax.rem(dp + down, ndp), lax.rem(me + step, n)), device_id_type=MESH
                )
    pl.semaphore_wait(barrier, n * ndp - 1)


def whole_kernel(
    n, ndp, parts, cuts, block, piece,
    seg_ref, q_ref, k_ref, v_ref, og_ref, w_hbm,
    attended_out, qg_ref, kg_ref, vg_ref, wg_out,
    heads_ref, grads_ref, attention_ref, result_ref, probs_ref, dscore_ref, turned, query_mask, key_mask,
    w_ref, og_all, att_t, att_all, grad_ref, psend_buf, precv_buf,
    xsend_buf, xrecv_buf, own_sum, chain_buf, outer_buf, middle_buf, wg_ref, att_sum,
    load_sem, send_sem, recv_sem, osend, orecv, gsend, grecv, asend, arecv, hsend, hrecv,
    psend, precv, xsend, xrecv, csend, crecv, mrecv, bsend, brecv, fsend, frecv, store_sem, wide_sem,
):
    me, dp = lax.axis_index("ctx"), lax.axis_index("dp")
    core = lax.rem(me, 2)
    chip = me // 2
    chips = n // 2
    sibling = me + 1 - 2 * core
    slots, _, seq, _ = heads_ref.shape
    rows = q_ref.shape[0]
    width = og_ref.shape[1]
    wrows = w_ref.shape[0]
    half = wrows // 2
    wide = width // parts
    broad = width // cuts
    pieces = wrows // piece
    scale = 1.0 / math.sqrt(HD)

    def record_rows(record):
        return pl.ds(pl.multiple_of(record * rows, rows), rows)

    my_rows = record_rows(me)
    loads = (
        pltpu.make_async_copy(w_hbm, w_ref, load_sem.at[0]),
        pltpu.make_async_copy(og_ref, og_all.at[record_rows(dp)], load_sem.at[1]),
    )
    for load in loads:
        load.start()
    greet(n, ndp)

    def head_columns(head):
        if isinstance(head, int):
            return pl.ds(head * HD, HD)
        return pl.ds(pl.multiple_of(head * HD, HD), HD)

    def place_of(head):
        slot = head // n
        place = head - slot * n
        if slots > 1:
            moved = 2 * place + 2
            place = jnp.where(jnp.logical_and(slot > 0, moved < n), moved, place)
        return place, slot

    def send_head(tensor, source, head, start):
        place, slot = owner_of(head, n)
        columns = head_columns(head)
        landing = heads_ref.at[slot, tensor, my_rows]
        copy = remote(
            source.at[:, columns], landing, send_sem.at[tensor, head], recv_sem.at[slot, tensor], dp, place,
        )

        @pl.when(me != place)
        def _():
            if start:
                copy.start()
            else:
                copy.wait_send()

        if start:
            @pl.when(me == place)
            def _():
                pltpu.make_async_copy(source.at[:, columns], landing, recv_sem.at[slot, tensor]).start()

    def await_head(slot, tensor):
        waited = heads_ref.at[slot, tensor]
        pltpu.make_async_copy(waited, waited, recv_sem.at[slot, tensor]).wait()

    def og_copy(source, at, count, record, slot, peer):
        landed = pl.ds(pl.multiple_of(record * rows + at, 16), count)
        return remote(source, og_all.at[landed], osend.at[slot], orecv.at[slot], peer, me)

    def send_slot(slot):
        for tensor, source in enumerate((q_ref, k_ref, v_ref)):
            for head in range(slot * n, min(HEADS, slot * n + n)):
                send_head(tensor, source, head, True)

    spread = []
    if ndp == 4:
        cut = rows // 2
        across = dp + 1 - 2 * lax.rem(dp, 2)
        along = lax.rem(dp + 2, 4)
        corner = 3 - dp
        peers = (across, along, corner)
        for order in range(2):
            for axis, peer in enumerate((across, along)):
                part = order if axis == 0 else 1 - order
                spread.append(
                    og_copy(og_ref.at[pl.ds(part * cut, cut)], part * cut, cut, dp, 2 * axis + part, peer)
                )
    else:
        peers = tuple(lax.rem(dp + ndp - step, ndp) for step in range(1, ndp))
        for step in range(1, ndp):
            spread.append(og_copy(og_ref, 0, rows, dp, step, lax.rem(dp + step, ndp)))
    for copy in spread:
        copy.start()
    send_slot(0)

    def piece_place(spot):
        feature = dp * wrows + spot * piece
        head = feature // HD
        place, slot = place_of(head)
        return place, slot, feature - head * HD

    def grad_copy(step, record, spot):
        place, slot, inside = piece_place(spot)
        return remote(
            grad_ref.at[step, pl.ds(spot * piece, piece)],
            grads_ref.at[slot, pl.ds(pl.multiple_of(inside, 16), piece), my_rows],
            gsend.at[step, spot], grecv.at[slot, inside // piece], record, place,
        )

    def make_grad(step, record):
        grad_ref[step] = dot_nt(w_ref[...], og_all[record_rows(record), :]).astype(BF16)

    def send_grad(step, record):
        for spot in range(pieces):
            if step:
                grad_copy(step, record, spot).start()
            else:
                place, slot, inside = piece_place(spot)

                @pl.when(place == me)
                def _():
                    held = pl.ds(pl.multiple_of(inside, 16), piece)
                    grads_ref[slot, held, my_rows] = grad_ref[0, pl.ds(spot * piece, piece), :]

                @pl.when(place != me)
                def _():
                    grad_copy(0, record, spot).start()

    for load in loads:
        load.wait()
    make_grad(0, dp)

    @pl.loop(0, seq // block)
    def _(index):
        at = pl.ds(pl.multiple_of(index * block, block), block)
        position = lax.broadcasted_iota(jnp.int32, (block, HD), 0) + index * block
        lane = lax.broadcasted_iota(jnp.int32, (block, HD), 1)
        count = seg_ref.shape[1]
        end = jnp.int32(0)
        segment = jnp.zeros((block, HD), jnp.int32)
        for i in range(count):
            end = end + seg_ref[0, i]
            segment = segment + jnp.where(position >= end, 1, 0)
        query_mask[at, :] = jnp.where(segment == lane, 1.0, 0.0).astype(BF16)
        key_mask[at, :] = jnp.where(jnp.logical_or(segment == lane, lane >= count), 0.0, MASKED_SCORE).astype(BF16)

    def await_og(slot, at, count, record):
        landed = og_all.at[pl.ds(pl.multiple_of(record * rows + at, 16), count)]
        remote(landed, landed, osend.at[0], orecv.at[slot], dp, me).wait_recv()
        return landed

    if ndp == 4:
        for axis, (peer, other) in enumerate(((across, along), (along, across))):
            landed = await_og(3 * axis, axis * cut, cut, peer)
            copy = og_copy(landed, axis * cut, cut, peer, 4 + axis, other)
            copy.start()
            spread.append(copy)
    for slot in range(1, slots):
        send_slot(slot)
    if ndp == 4:
        for axis, peer in enumerate((across, along)):
            await_og(axis + 1, (1 - axis) * cut, cut, peer)
            make_grad(axis + 1, peer)
    else:
        for step, peer in enumerate(peers, 1):
            await_og(step, 0, rows, peer)
            make_grad(step, peer)

    def attention_copy(slot, other, spot):
        head, _ = head_in_slot(me, slot, n)
        feature = head * HD + spot * piece
        target = feature // wrows
        row = feature - target * wrows
        landing = att_t.at[pl.ds(pl.multiple_of(row, 16), piece), record_rows(dp)]
        return target, landing, remote(
            attention_ref.at[slot, pl.ds(spot * piece, piece), record_rows(other)], landing,
            asend.at[slot, other, spot], arecv.at[dp, row // piece], target, other,
        )

    def attention_copies(slot, other, start):
        for spot in range(HD // piece):
            target, landing, copy = attention_copy(slot, other, spot)
            here = jnp.logical_and(target == dp, other == me)

            @pl.when(jnp.logical_not(here))
            def _():
                if start:
                    copy.start()
                else:
                    copy.wait_send()

            if start:
                @pl.when(here)
                def _():
                    landing[...] = attention_ref[slot, pl.ds(spot * piece, piece), my_rows]

    log2e = math.log2(math.e)

    def forward(slot):
        @pl.when(head_in_slot(me, slot, n)[1])
        def _():
            for tensor in range(3):
                await_head(slot, tensor)
            turned[...] = heads_ref[slot, 2].T

            @pl.loop(0, seq // block)
            def _(index):
                at = pl.ds(pl.multiple_of(index * block, block), block)
                left = jnp.concatenate([heads_ref[slot, 1], key_mask[...]], axis=1)
                right = jnp.concatenate([heads_ref[slot, 0, at, :], query_mask[at, :]], axis=1)
                scores = dot_nt(left, right)
                top = jnp.max(scores, axis=0, keepdims=True)
                shifted = jnp.exp2((scores - top) * (scale * log2e))
                total = jnp.sum(shifted, axis=0, keepdims=True)
                probs_b = (shifted * (1.0 / total)).astype(BF16)
                probs_ref[slot, :, at] = probs_b
                attention_ref[slot, :, at] = dot_nn(turned[...], probs_b).astype(BF16)
                for step in range(block // rows):
                    attention_copies(slot, index * (block // rows) + step, True)

    targets = (qg_ref, kg_ref, vg_ref)

    def home_copy(slot, tensor, other):
        head, _ = head_in_slot(me, slot, n)
        return remote(
            result_ref.at[slot, tensor, record_rows(other)], targets[tensor].at[:, head_columns(head)],
            hsend.at[tensor, slot, other], hrecv.at[tensor, head], dp, other,
        )

    def send_home(slot, tensor, other):
        @pl.when(other != me)
        def _():
            home_copy(slot, tensor, other).start()

        @pl.when(other == me)
        def _():
            head, _ = head_in_slot(me, slot, n)
            landing = targets[tensor].at[:, head_columns(head)]
            pltpu.make_async_copy(result_ref.at[slot, tensor, my_rows], landing, hrecv.at[tensor, head]).start()

    def receive_home(tensor):
        for head in range(HEADS):
            landed = targets[tensor].at[:, head_columns(head)]
            pltpu.make_async_copy(landed, landed, hrecv.at[tensor, head]).wait()

    def backward(slot):
        @pl.when(head_in_slot(me, slot, n)[1])
        def _():
            head, _ = head_in_slot(me, slot, n)
            turned[...] = heads_ref[slot, 1].T
            for spot in range(HD // piece):
                source = (head * HD + spot * piece) // wrows

                def await_grad(count):
                    waited = grads_ref.at[slot, pl.ds(spot * piece, piece), pl.ds(0, rows * count)]
                    pltpu.make_async_copy(waited, waited, grecv.at[slot, spot]).wait()

                pl.when(source == dp)(lambda: await_grad(n - 1))
                pl.when(source != dp)(lambda: await_grad(n))

            @pl.loop(0, seq // block)
            def _(index):
                at = pl.ds(pl.multiple_of(index * block, block), block)
                result_ref[slot, 2, at, :] = dot_nt(probs_ref[slot, at, :], grads_ref[slot]).astype(BF16)
                for step in range(block // rows):
                    send_home(slot, 2, index * (block // rows) + step)

            @pl.loop(0, seq // block)
            def _(index):
                at = pl.ds(pl.multiple_of(index * block, block), block)
                grad = grads_ref[slot, :, at]
                product = grad.astype(F32) * attention_ref[slot, :, at].astype(F32)
                grad_dot = jnp.sum(product, axis=0, keepdims=True)
                dprob = dot_nn(heads_ref[slot, 2], grad)
                dscore = (probs_ref[slot, :, at].astype(F32) * (dprob - grad_dot)).astype(BF16)
                dscore_ref[:, at] = dscore
                result_ref[slot, 0, at, :] = (dot_nn(turned[...], dscore) * scale).astype(BF16).T

            @pl.loop(0, seq // block)
            def _(index):
                at = pl.ds(pl.multiple_of(index * block, block), block)
                result_ref[slot, 1, at, :] = (dot_nn(dscore_ref[at, :], heads_ref[slot, 0]) * scale).astype(BF16)

    def send_some(slot, tensor, others):
        @pl.when(head_in_slot(me, slot, n)[1])
        def _():
            for other in others:
                send_home(slot, tensor, other)

    for slot in range(slots):
        forward(slot)
    for step, record in enumerate((dp,) + peers[:2]):
        send_grad(step, record)
    if ndp == 4:
        for axis in range(2):
            await_og(4 + axis, axis * cut, cut, corner)
        make_grad(3, corner)
    for step, record in enumerate(peers[2:], 3):
        send_grad(step, record)

    for record in range(ndp):
        for spot in range(pieces):
            landed = att_t.at[pl.ds(spot * piece, piece), pl.ds(record * rows, rows)]
            here = jnp.logical_and(record == dp, piece_place(spot)[0] == me)

            @pl.when(jnp.logical_not(here))
            def _():
                remote(landed, landed, asend.at[0, 0, 0], arecv.at[record, spot], dp, sibling).wait_recv()

    def part_columns(part):
        return pl.ds(part * wide, wide)

    def cut_columns(part):
        return pl.ds(part * broad, broad)

    my_half = pl.ds(pl.multiple_of(core * half, 16), half)
    their_half = pl.ds(pl.multiple_of((1 - core) * half, 16), half)

    def pair_copy(part):
        columns = cut_columns(part)
        return remote(
            xsend_buf.at[:, columns], xrecv_buf.at[:, columns], xsend.at[part], xrecv.at[part], dp, sibling,
        )

    def partial_copy(part, step, source, other):
        columns = cut_columns(part)
        return remote(
            psend_buf.at[record_rows(source), columns], precv_buf.at[step - 1, :, columns],
            psend.at[part, step], precv.at[part, step], other, me,
        )

    def partial_copies(part):
        if ndp == 4:
            near, far = (across, along) if 2 * part < cuts else (along, across)
            moves = ((near, near), (corner, near), (far, far))
        else:
            moves = tuple((lax.rem(dp + step, ndp),) * 2 for step in range(1, ndp))
        return tuple(functools.partial(partial_copy, part, step, *move) for step, move in enumerate(moves, 1))

    def partial_relay(part):
        far = along if 2 * part < cuts else across
        columns = cut_columns(part)
        copies = partial_copies(part)
        copies[1]().wait_recv()
        held = record_rows(far)
        total = psend_buf[held, columns].astype(F32) + precv_buf[1, :, columns].astype(F32)
        psend_buf[held, columns] = total.astype(BF16)
        copies[2]().start()

    for part in range(cuts):
        columns = cut_columns(part)
        product = dot_nn(att_t[...], og_all[:, columns])
        low, high = product[:half], product[half:]
        xsend_buf[:, columns] = jnp.where(core == 0, high, low).astype(BF16)
        own_sum[:, columns] = jnp.where(core == 0, low, high)
        pair_copy(part).start()
    att_all[...] = att_t[...].T
    order = [part for pair in zip(range(cuts // 2), range(cuts // 2, cuts)) for part in pair]
    for part in order:
        columns = cut_columns(part)
        psend_buf[:, columns] = dot_nn(att_all[...], w_ref[:, columns]).astype(BF16)
        for copy in partial_copies(part)[: 2 if ndp == 4 else ndp]:
            copy().start()
    depth = jnp.where(chip < chips // 2, chip, chips - 1 - chip)
    toward = jnp.where(chip < chips // 2, 1, -1)
    innermost = depth == chips // 2 - 1
    inner = me + 2 * toward
    outer = me - 2 * toward

    def inward_copy(part):
        columns = part_columns(part)
        return remote(
            chain_buf.at[:, columns], outer_buf.at[:, columns], csend.at[part], crecv.at[part], dp, inner,
        )

    def middle_copy(part):
        columns = part_columns(part)
        return remote(
            chain_buf.at[:, columns], middle_buf.at[:, columns], csend.at[part], mrecv.at[part], dp, inner,
        )

    def outward_copy(part):
        landed = wg_ref.at[:, part_columns(part)]
        return remote(landed, landed, bsend.at[part], brecv.at[part], dp, outer)

    def pass_copy(part, held):
        columns = part_columns(part)
        return remote(wg_ref.at[:, columns], wg_out.at[held, columns], fsend.at[part], frecv.at[part], dp, sibling)

    def wide_store(part):
        columns = part_columns(part)
        return pltpu.make_async_copy(wg_ref.at[:, columns], wg_out.at[my_half, columns], wide_sem.at[part])

    def store(part):
        columns = cut_columns(part)
        return pltpu.make_async_copy(att_sum.at[:, columns], attended_out.at[:, columns], store_sem.at[part])

    def hand_on(part):
        @pl.when(depth > 0)
        def _():
            outward_copy(part).start()

        pass_copy(part, my_half).start()
        wide_store(part).start()

    def finish_inner(part):
        columns = part_columns(part)
        middle_copy(part).wait_recv()
        total = chain_buf[:, columns].astype(F32) + middle_buf[:, columns].astype(F32)
        wg_ref[:, columns] = total.astype(BF16)
        hand_on(part)

    def chain_sum(part):
        columns = part_columns(part)
        for waited in range(cuts):
            if part * wide <= waited * broad < (part + 1) * wide:
                pair_copy(waited).wait_recv()
        own_sum[:, columns] += xrecv_buf[:, columns].astype(F32)

        @pl.when(depth > 0)
        def _():
            inward_copy(part).wait_recv()
            own_sum[:, columns] += outer_buf[:, columns].astype(F32)

        chain_buf[:, columns] = own_sum[:, columns].astype(BF16)

    @pl.when(jnp.logical_not(innermost))
    def _():
        for part in range(parts):
            chain_sum(part)
            inward_copy(part).start()

    for slot in range(slots):
        backward(slot)
        send_some(slot, 0, range(n))

    lag = 4

    @pl.when(innermost)
    def _():
        for part in range(parts):
            chain_sum(part)
            if part >= lag:
                middle_copy(part - lag).wait_send()
            middle_copy(part).start()
            if part >= lag:
                finish_inner(part - lag)
            for slot in range(slots):
                send_some(slot, 1, range(part * n // parts, (part + 1) * n // parts))
            if ndp == 4 and 3 <= part < 3 + cuts:
                partial_relay(order[part - 3])
        for part in range(parts - lag, parts):
            finish_inner(part)

    @pl.when(jnp.logical_not(innermost))
    def _():
        for slot in range(slots):
            send_some(slot, 1, range(n))
        if ndp == 4:
            for part in order:
                partial_relay(part)

    for part in order:
        columns = cut_columns(part)
        total = psend_buf[record_rows(dp), columns].astype(F32)
        for step, copy in enumerate(partial_copies(part)):
            if ndp != 4 or step != 1:
                copy().wait_recv()
                total = total + precv_buf[step, :, columns].astype(F32)
        att_sum[:, columns] = total.astype(BF16)
        store(part).start()

    for part in range(parts):
        @pl.when(jnp.logical_not(innermost))
        def _():
            outward_copy(part).wait_recv()
            hand_on(part)

    for tensor in range(3):
        receive_home(tensor)
    for part in range(parts):
        pass_copy(part, their_half).wait_recv()

    for tensor, source in enumerate((q_ref, k_ref, v_ref)):
        for head in range(HEADS):
            send_head(tensor, source, head, False)
    for copy in spread:
        copy.wait_send()
    for step, record in enumerate((dp,) + peers):
        for spot in range(pieces):
            copy = grad_copy(step, record, spot)
            if step:
                copy.wait_send()
            else:
                pl.when(piece_place(spot)[0] != me)(copy.wait_send)
    for slot in range(slots):
        @pl.when(head_in_slot(me, slot, n)[1])
        def _():
            for other in range(n):
                attention_copies(slot, other, False)
                for tensor in range(3):
                    pl.when(other != me)(home_copy(slot, tensor, other).wait_send)
    for part in range(cuts):
        pair_copy(part).wait_send()
        for copy in partial_copies(part):
            copy().wait_send()
    for part in range(parts):
        if part >= parts - lag:
            inward_copy(part).wait_send()
        else:
            pl.when(jnp.logical_not(innermost))(inward_copy(part).wait_send)
        pl.when(depth > 0)(outward_copy(part).wait_send)
        pass_copy(part, my_half).wait_send()
        wide_store(part).wait()
    for part in range(cuts):
        store(part).wait()


def copy_kernel(pieces, *refs):
    sources, targets, held = refs[:5], refs[5:10], refs[10:15]
    wide_held, in_sem, out_sem = refs[15:]
    spans = []
    for i in (4, 0, 1, 2, 3):
        rows = held[i].shape[0] // (pieces if i == 4 else 2)
        spans += [(i, pl.ds(at, rows)) for at in range(0, held[i].shape[0], rows)]
    loads = [pltpu.make_async_copy(sources[i].at[x], held[i].at[x], in_sem.at[j]) for j, (i, x) in enumerate(spans)]
    stores = [
        pltpu.make_async_copy((held[i] if i < 4 else wide_held).at[x], targets[i].at[x], out_sem.at[j])
        for j, (i, x) in enumerate(spans)
    ]
    for load in loads:
        load.start()
    for j, (i, x) in enumerate(spans):
        loads[j].wait()
        if i == 4:
            wide_held[x, :] = held[4][x, :].astype(F32)
        stores[j].start()
    for store in stores:
        store.wait()


def local(queries, keys, values, seg_lengths, out_grad, w_out):
    n, ndp = lax.axis_size("ctx"), lax.axis_size("dp")
    rows, inner = queries.shape[1:]
    width = out_grad.shape[2]
    seq = rows * n
    wrows = w_out.shape[0]
    half = wrows // 2
    slots = -(-HEADS // n)
    parts, cuts = 10, 4
    block = math.gcd(512, seq)
    piece = math.gcd(HD, wrows)
    shape = jax.ShapeDtypeStruct
    dma = pltpu.SemaphoreType.DMA
    out_shape = (
        shape((rows, width), BF16), shape((rows, inner), BF16), shape((rows, inner), BF16),
        shape((rows, inner), BF16), shape((wrows, width), F32),
    )
    anywhere = [pl.BlockSpec(memory_space=pl.ANY)] * 5
    outputs = pl.pallas_call(
        functools.partial(whole_kernel, n, ndp, parts, cuts, block, piece),
        out_shape=out_shape[:4] + (shape((wrows, width), BF16),),
        in_specs=[pl.BlockSpec(memory_space=pltpu.SMEM)] + anywhere,
        out_specs=tuple(anywhere),
        scratch_shapes=[
            pltpu.VMEM((slots, 3, seq, HD), BF16),
            pltpu.VMEM((slots, HD, seq), BF16),
            pltpu.VMEM((slots, HD, seq), BF16),
            pltpu.VMEM((slots, 3, seq, HD), BF16),
            pltpu.VMEM((slots, seq, seq), BF16),
            pltpu.VMEM((seq, seq), BF16),
            pltpu.VMEM((HD, seq), BF16),
            pltpu.VMEM((seq, HD), BF16),
            pltpu.VMEM((seq, HD), BF16),
            pltpu.VMEM((wrows, width), BF16),
            pltpu.VMEM((ndp * rows, width), BF16),
            pltpu.VMEM((wrows, ndp * rows), BF16),
            pltpu.VMEM((ndp * rows, wrows), BF16),
            pltpu.VMEM((ndp, wrows, rows), BF16),
            pltpu.VMEM((ndp * rows, width), BF16),
            pltpu.VMEM((ndp - 1, rows, width), BF16),
            pltpu.VMEM((half, width), BF16),
            pltpu.VMEM((half, width), BF16),
            pltpu.VMEM((half, width), F32),
            pltpu.VMEM((half, width), BF16),
            pltpu.VMEM((half, width), BF16),
            pltpu.VMEM((half, width), BF16),
            pltpu.VMEM((half, width), BF16),
            pltpu.VMEM((rows, width), BF16),
            dma((2,)), dma((3, HEADS)), dma((slots, 3)), dma((max(ndp, 6),)), dma((max(ndp, 6),)),
            dma((ndp, wrows // piece)), dma((slots, HD // piece)), dma((slots, n, HD // piece)), dma((ndp, wrows // piece)),
            dma((3, slots, n)), dma((3, HEADS)),
            dma((cuts, ndp)), dma((cuts, ndp)), dma((cuts,)), dma((cuts,)),
            dma((parts,)), dma((parts,)), dma((parts,)), dma((parts,)), dma((parts,)), dma((parts,)), dma((parts,)),
            dma((cuts,)), dma((parts,)),
        ],
        compiler_params=pltpu.CompilerParams(
            collective_id=0, has_side_effects=True, vmem_limit_bytes=VMEM_BYTES
        ),
    )(seg_lengths, queries[0], keys[0], values[0], out_grad[0], w_out)
    attended, query_grad, key_grad, value_grad, weight_grad = pl.pallas_call(
        functools.partial(copy_kernel, 10),
        out_shape=out_shape,
        in_specs=anywhere,
        out_specs=tuple(anywhere),
        scratch_shapes=[pltpu.VMEM(x.shape, BF16) for x in out_shape]
        + [pltpu.VMEM((wrows, width), F32), dma((18,)), dma((18,))],
        compiler_params=pltpu.CompilerParams(vmem_limit_bytes=VMEM_BYTES),
    )(*outputs)
    return (attended[None], query_grad[None], key_grad[None], value_grad[None], weight_grad)


def solution(mesh):
    in_specs = (
        P("dp", "ctx", None),
        P("dp", "ctx", None),
        P("dp", "ctx", None),
        P("dp", None),
        P("dp", "ctx", None),
        P("dp", None),
    )
    out_specs = (
        P("dp", "ctx", None),
        P("dp", "ctx", None),
        P("dp", "ctx", None),
        P("dp", "ctx", None),
        P("dp", None),
    )
    return jax.shard_map(local, mesh=mesh, in_specs=in_specs, out_specs=out_specs, check_vma=False)
```
